128 devices in a mesh: rows: 16 (over x, y_hi, core), frames: 8 (over y_lo, z).
Axes of the slice: x: 4, y: 4 (y_hi: 2, y_lo: 2; y = y_hi * 2 + y_lo), z: 4, core: 2. Of those that a mesh axis runs over, the one named last changes fastest.
Arguments:
- latent: bfloat16 [128, 1664, 256], P('frames', 'rows'), may hold values from -25 to 25
- conv_weight: bfloat16 [4, 256, 256], replicated, may hold values from -0.25 to 0.25
- norm_gain: bfloat16 [256], replicated, may hold values from 0.099609375 to 1.8984375
- frame_embed: bfloat16 [256, 256], P('frames'), may hold values from -3 to 3
- qkv_weight: bfloat16 [256, 768], replicated, may hold values from -3 to 3
- out_weight: bfloat16 [256, 256], replicated, may hold values from -0.375 to 0.375
Outputs:
- blended: bfloat16 [256, 1664, 256], P('frames', 'rows')
The draws below stay inside these ranges and needn't reach their ends.
All inputs are finite; a program needn't handle non-finite values.
Results may differ from the reference program's by a relative error of at most 0.0095.
The reference program's roundings to bfloat16 on the way (of `upsampled`, `normed`, `projected`, `probabilities` and `context`) count: a program that leaves them out, or rounds other values in their place, can miss the bound.
Values may be sent and summed in bfloat16 or wider, within the bound.
No kernel may reach another device: no remote copies, remote signals or barrier semaphores. Data moves between devices by JAX's collectives and lax.ppermute only.
A program may use at most 64 MiB of HBM per device.

```python
import math
import jax
import jax.numpy as jnp
from jax import lax

C = 256
HEAD_DIM = 64
GROUPS = 32
PIX_DEV = 104
FRAMES_IN = 128
FRAMES_OUT = 256
PIXELS = 1664
N_ROWS = 16


def draw_latent(key, part):
    key = jax.random.fold_in(key, 11)
    key_base, key_frame, key_pixel, key_offset = jax.random.split(key, 4)
    frame_pos = jnp.arange(FRAMES_IN, dtype=jnp.float32) / FRAMES_IN
    pixel_pos = jnp.arange(PIXELS, dtype=jnp.float32) / PIXELS
    frame_scale = jnp.exp(math.log(3.0) * frame_pos + jax.random.uniform(key_frame, (FRAMES_IN,), jnp.float32, 0.0, math.log(1.8)))
    pixel_rise = math.log(3.0)
    offset = jax.random.uniform(key_offset, (C,), jnp.float32, 0.4, 1.0)
    base = jnp.clip(jax.random.normal(key_base, (FRAMES_IN, PIXELS, C), jnp.float32), -4.0, 4.0)
    pixel_scale = jnp.exp(pixel_rise * pixel_pos + jax.random.uniform(key_pixel, (PIXELS,), jnp.float32, 0.0, math.log(1.8)))
    values = 0.16 * (base + offset[None, None, :]) * frame_scale[:, None, None] * pixel_scale[None, :, None]
    return values.astype(jnp.bfloat16)


def draw_qkv_weight(key, part):
    key = jax.random.fold_in(key, 12)
    key_query, key_key, key_value = jax.random.split(key, 3)
    deviation = C ** (-0.5)
    main = jnp.clip(jax.random.normal(key_query, (C, C), jnp.float32), -4.0, 4.0) * deviation
    other = jnp.clip(jax.random.normal(key_key, (C, C), jnp.float32), -4.0, 4.0) * deviation
    value_part = jnp.clip(jax.random.normal(key_value, (C, C), jnp.float32), -4.0, 4.0) * deviation
    query_part = main
    key_part = other
    return jnp.concatenate([query_part, key_part, value_part], axis=1).astype(jnp.bfloat16)


def block_scale(key, extent, pieces, smallest, top_value):
    loudness = 1.0
    for axis_at, shards_of in pieces:
        heights = jax.random.uniform(jax.random.fold_in(jax.random.fold_in(key, 6), axis_at), (shards_of,), jnp.float32, smallest / len(pieces), top_value / len(pieces))
        loudness = loudness * jnp.repeat(jnp.exp(heights), extent[axis_at] // shards_of).reshape((-1,) + (1,) * (len(extent) - 1 - axis_at))
    return loudness


def noise(key, shape, width, reach, cuts=(), held_as=jnp.bfloat16):
    entries = width * jax.random.normal(key, shape, jnp.float32)
    if cuts:
        entries = entries * block_scale(key, shape, cuts, -0.22, 0.18)
    return jnp.clip(entries, -reach, reach).astype(held_as)


def setup_inputs(seed: int = 0) -> dict:
    key_list = jax.random.split(jax.random.key(seed), 7)
    latent = draw_latent(jax.random.fold_in(key_list[6], 71), 0)
    conv_weight = noise(key_list[1], (4, C, C), (2 * C) ** -0.5, 0.25)
    norm_gain = jnp.clip(1.0 + 0.18 * jax.random.normal(key_list[2], (C,), jnp.float32), 0.099609375, 1.8984375).astype(jnp.bfloat16)
    frame_embed = noise(key_list[3], (FRAMES_OUT, C), 0.5, 3.0, ((0, 8),))
    qkv_weight = draw_qkv_weight(jax.random.fold_in(key_list[6], 71), 0)
    out_weight = noise(key_list[5], (C, C), C ** -0.5, 0.375)
    return {"latent": latent, "conv_weight": conv_weight, "norm_gain": norm_gain, "frame_embed": frame_embed, "qkv_weight": qkv_weight, "out_weight": out_weight}


epsilon = 1e-06
highest = lax.Precision.HIGHEST

def project(values, weight):
    return jnp.einsum('...c,cd->...d', values.astype(jnp.float32), weight.astype(jnp.float32), precision=highest)

def upsample_block(pixel_block, conv_weight):
    padded = jnp.pad(pixel_block, ((1, 1), (0, 0), (0, 0)))
    length = pixel_block.shape[0]
    even_frames = project(padded[1:length + 1], conv_weight[1]) + project(padded[0:length], conv_weight[3])
    odd_frames = project(padded[2:length + 2], conv_weight[0]) + project(padded[1:length + 1], conv_weight[2])
    stacked = jnp.stack([even_frames, odd_frames], axis=1)
    return stacked.reshape((2 * length,) + pixel_block.shape[1:]).astype(jnp.bfloat16)

def attend_pixel(projected):
    channels = projected.shape[-1] // 3
    length = projected.shape[0]
    queries = projected[:, :channels].reshape(length, channels // HEAD_DIM, HEAD_DIM).astype(jnp.float32)
    keys = projected[:, channels:2 * channels].reshape(length, channels // HEAD_DIM, HEAD_DIM).astype(jnp.float32)
    values = projected[:, 2 * channels:].reshape(length, channels // HEAD_DIM, HEAD_DIM).astype(jnp.float32)
    scores = jnp.einsum('qhd,khd->hqk', queries, keys, precision=highest) * HEAD_DIM ** (-0.5)
    scores = scores - lax.optimization_barrier(jnp.max(scores, axis=-1, keepdims=True))
    weights = jnp.exp(scores)
    probabilities = (weights / lax.optimization_barrier(jnp.sum(weights, axis=-1, keepdims=True))).astype(jnp.bfloat16)
    context = jnp.einsum('hqk,khd->qhd', probabilities.astype(jnp.float32), values, precision=highest)
    return context.reshape(length, channels).astype(jnp.bfloat16)

def reference(latent, conv_weight, norm_gain, frame_embed, qkv_weight, out_weight):
    blocks = jnp.moveaxis(latent.reshape(FRAMES_IN, N_ROWS, PIX_DEV, C), 1, 0)
    upsampled = lax.map(lambda pixel_block: upsample_block(pixel_block, conv_weight), blocks)
    group_size = C // GROUPS
    counted = FRAMES_OUT * PIXELS * group_size

    def group_sums(pixel_block):
        return lax.optimization_barrier(jnp.sum(pixel_block.astype(jnp.float32), axis=(0, 1))).reshape(GROUPS, group_size).sum(axis=1)
    center = lax.optimization_barrier(jnp.sum(lax.map(group_sums, upsampled), axis=0)) / counted
    channel_center = jnp.repeat(center, group_size)

    def group_spread(pixel_block):
        deviation = pixel_block.astype(jnp.float32) - channel_center
        return lax.optimization_barrier(jnp.sum(deviation * deviation, axis=(0, 1))).reshape(GROUPS, group_size).sum(axis=1)
    variance = lax.optimization_barrier(jnp.sum(lax.map(group_spread, upsampled), axis=0)) / counted
    channel_scale = jnp.repeat(lax.rsqrt(variance + epsilon), group_size) * norm_gain.astype(jnp.float32)

    def layer(pixel_block):
        upsampled_float = pixel_block.astype(jnp.float32)
        normed = ((upsampled_float - channel_center) * channel_scale + frame_embed.astype(jnp.float32)[:, None, :]).astype(jnp.bfloat16)
        projected = project(normed, qkv_weight).astype(jnp.bfloat16)
        per_pixel = jnp.moveaxis(projected, 1, 0)
        context = lax.map(attend_pixel, per_pixel, batch_size=16)
        context = jnp.moveaxis(context, 0, 1)
        blended = upsampled_float + project(context, out_weight)
        return blended.astype(jnp.bfloat16)
    result = lax.map(layer, upsampled)
    return jnp.moveaxis(result, 0, 1).reshape(FRAMES_OUT, PIXELS, C)
```

```python
import functools

import jax
import jax.numpy as jnp
from jax import lax
from jax.experimental import pallas as pl
from jax.experimental.pallas import tpu as pltpu
from jax.sharding import PartitionSpec as P

HEAD_DIM = 64
GROUPS = 32
EPSILON = 1e-06
LANES = 128
LOG2E = 1.4426950408889634
HIGHEST = lax.Precision.HIGHEST
BF16 = jnp.bfloat16
F32 = jnp.float32
NT = (((1,), (1,)), ((), ()))


def params(mib):
    return pltpu.CompilerParams(vmem_limit_bytes=mib * 1024 * 1024)


def pack_kernel(latent_ref, embed_ref, out_ref, wide, embed_wide):
    frames, pixels, _ = latent_ref.shape
    devices = out_ref.shape[0]
    share = pixels // devices
    for half in range(wide.shape[0]):
        lanes = slice(half * LANES, (half + 1) * LANES)
        for f in range(frames):
            wide[half, f * pixels : (f + 1) * pixels, :] = latent_ref[f, :, lanes].astype(F32)
        embed_wide[half] = embed_ref[:, lanes].astype(F32)
        for p in range(pixels):
            d, j = divmod(p, share)
            rows = wide[half, pl.ds(p, frames, stride=pixels), :].astype(BF16)
            out_ref[d, j * frames : (j + 1) * frames, lanes] = rows
        for parity in range(2):
            rows = embed_wide[half, pl.ds(parity, frames, stride=2), :].astype(BF16)
            base = share * frames + parity * frames
            for d in range(devices):
                out_ref[d, base : base + frames, lanes] = rows


def pack(latent, frame_embed, devices):
    frames, pixels, channels = latent.shape
    rows = pixels // devices * frames + 2 * frames
    return pl.pallas_call(
        pack_kernel,
        out_shape=jax.ShapeDtypeStruct((devices, rows, channels), BF16),
        scratch_shapes=[
            pltpu.VMEM((channels // LANES, frames * pixels, LANES), F32),
            pltpu.VMEM((channels // LANES, 2 * frames, LANES), F32),
        ],
        compiler_params=params(24),
        name="pack_latent",
    )(latent, frame_embed)


def group_matrix(channels, offset):
    size = channels // GROUPS
    channel = lax.broadcasted_iota(jnp.int32, (channels, LANES), 0)
    lane = lax.broadcasted_iota(jnp.int32, (channels, LANES), 1)
    return jnp.where(channel // size + offset == lane, 1.0, 0.0).astype(F32)


def group_spread(channels):
    size = channels // GROUPS
    lane = lax.broadcasted_iota(jnp.int32, (LANES, channels), 0)
    channel = lax.broadcasted_iota(jnp.int32, (LANES, channels), 1)
    return jnp.where(channel // size == lane, 1.0, 0.0).astype(F32)


def exact_dot(a, b):
    return jnp.dot(a, b, precision=HIGHEST, preferred_element_type=F32)


def upsample_kernel(share, block_ref, conv_ref, up_ref, stats_ref, taps):
    devices = block_ref.shape[0]
    channels = block_ref.shape[2]
    part = (block_ref.shape[1]) // (share + 2)
    length = devices * part
    row = lax.broadcasted_iota(jnp.int32, (length, channels), 0)
    for j in range(share):
        here = jnp.concatenate([block_ref[s, j * part : (j + 1) * part, :] for s in range(devices)], axis=0)
        wide = here.astype(F32)
        before = jnp.where(row == 0, 0.0, pltpu.roll(wide, 1, 0))
        after = jnp.where(row == length - 1, 0.0, pltpu.roll(wide, length - 1, 0))
        rows = slice(j * length, (j + 1) * length)
        taps[0, rows, :] = before.astype(BF16)
        taps[1, rows, :] = here
        taps[2, rows, :] = after.astype(BF16)

    def tap(source, index):
        return jnp.dot(taps[source], conv_ref[index], preferred_element_type=F32)

    even = (tap(1, 1) + tap(0, 3)).astype(BF16)
    odd = (tap(2, 0) + tap(1, 2)).astype(BF16)
    for j in range(share):
        up_ref[j, 0] = even[j * length : (j + 1) * length]
        up_ref[j, 1] = odd[j * length : (j + 1) * length]
    count = share * 2 * length * (channels // GROUPS)
    total = jnp.zeros((8, channels), F32)

    def add_rows(i, total):
        chunk = up_ref[i].astype(F32).reshape(-1, 8, channels)
        return total + jnp.sum(chunk, axis=0)

    total = lax.fori_loop(0, share, add_rows, total)
    total = jnp.broadcast_to(jnp.sum(total, axis=0, keepdims=True), (8, channels))
    mean = exact_dot(total, group_matrix(channels, 0)) / count
    center = exact_dot(mean, group_spread(channels))[0:1]

    def add_squares(i, spread):
        away = (up_ref[i].astype(F32).reshape(-1, channels) - center).reshape(-1, 8, channels)
        return spread + jnp.sum(away * away, axis=0)

    spread = lax.fori_loop(0, share, add_squares, jnp.zeros((8, channels), F32))
    spread = jnp.broadcast_to(jnp.sum(spread, axis=0, keepdims=True), (8, channels))
    stats_ref[...] = (mean + exact_dot(spread, group_matrix(channels, LANES // 2)))[0:1]


def upsample(block, conv_weight, share):
    devices, rows, channels = block.shape
    length = devices * (rows // (share + 2))
    return pl.pallas_call(
        functools.partial(upsample_kernel, share),
        out_shape=(
            jax.ShapeDtypeStruct((share, 2, length, channels), BF16),
            jax.ShapeDtypeStruct((1, LANES), F32),
        ),
        scratch_shapes=[pltpu.VMEM((3, share * length, channels), BF16)],
        compiler_params=params(48),
        name="upsample",
    )(block, conv_weight)


def attend_kernel(
    count, up_ref, stats_ref, gain_ref, block_ref, qkv_ref, out_weight_ref, out_ref, embed, wq_t, wv_t
):
    share, _, length, channels = up_ref.shape
    devices = block_ref.shape[0]
    part = length // devices
    frames = 2 * length
    heads = channels // HEAD_DIM
    per_lane = LANES // HEAD_DIM

    stats = stats_ref[...].reshape(-1, LANES)
    holders = stats.shape[0]
    center = jnp.sum(stats, axis=0, keepdims=True) / holders
    away = stats - center
    between = jnp.sum(away * away, axis=0, keepdims=True) * count
    within = pltpu.roll(center, LANES // 2, 1) * holders
    lane = lax.broadcasted_iota(jnp.int32, (1, LANES), 1)
    variance = jnp.where(lane < GROUPS, (between + within) / (count * holders), 0.0)
    center = jnp.where(lane < GROUPS, center, 0.0)
    moments = jnp.concatenate(
        [jnp.broadcast_to(center, (8, LANES)), jnp.broadcast_to(variance, (8, LANES))], axis=0
    )
    moments = exact_dot(moments, group_spread(channels))
    center = moments[0:1]
    scale = lax.rsqrt(moments[8:9] + EPSILON) * gain_ref[...].astype(F32)

    base = share * part
    for parity in range(2):
        for s in range(devices):
            start = base + parity * part
            embed[parity * length + s * part : parity * length + (s + 1) * part, :] = block_ref[
                s, start : start + part, :
            ].astype(F32)
    wq_t[...] = qkv_ref[:, 0:channels].astype(F32).T.astype(BF16)
    wv_t[...] = qkv_ref[:, 2 * channels : 3 * channels].astype(F32).T.astype(BF16)
    empty = jnp.zeros((HEAD_DIM, frames), BF16)

    def one_pixel(j, carry):
        up = up_ref[j].reshape(frames, channels).astype(F32)
        normed = ((up - center) * scale + embed[...]).astype(BF16)
        keys = jnp.dot(normed, qkv_ref[:, channels : 2 * channels], preferred_element_type=F32).astype(BF16)
        queries_t = lax.dot_general(wq_t[...], normed, NT, preferred_element_type=F32).astype(BF16)
        values_t = lax.dot_general(wv_t[...], normed, NT, preferred_element_type=F32).astype(BF16)
        context_t = []
        for h in range(heads):
            pair, place = divmod(h, per_lane)
            query = queries_t[h * HEAD_DIM : (h + 1) * HEAD_DIM, :]
            query = jnp.concatenate([query if i == place else empty for i in range(per_lane)], axis=0)
            scores = jnp.dot(keys[:, pair * LANES : (pair + 1) * LANES], query, preferred_element_type=F32)
            top = jnp.max(scores, axis=0, keepdims=True)
            weights = jnp.exp2((scores - top) * (LOG2E * HEAD_DIM**-0.5))
            total = jnp.sum(weights, axis=0, keepdims=True)
            probabilities = (weights * (1.0 / total)).astype(BF16)
            context_t.append(
                jnp.dot(
                    values_t[h * HEAD_DIM : (h + 1) * HEAD_DIM, :], probabilities, preferred_element_type=F32
                )
            )
        context = jnp.concatenate(context_t, axis=0).T.astype(BF16)
        mixed = jnp.dot(context, out_weight_ref[...], preferred_element_type=F32)
        blended = (up + mixed).astype(BF16)
        for d in range(devices):
            for parity in range(2):
                out_ref[d, j, parity] = blended[parity * length + d * part : parity * length + (d + 1) * part]
        return carry

    lax.fori_loop(0, share, one_pixel, 0)


def attend(up, stats, norm_gain, block, qkv_weight, out_weight):
    share, _, length, channels = up.shape
    devices = block.shape[0]
    part = length // devices
    count = share * 2 * length * (channels // GROUPS)
    return pl.pallas_call(
        functools.partial(attend_kernel, count),
        out_shape=jax.ShapeDtypeStruct((devices, share, 2, part, channels), BF16),
        scratch_shapes=[
            pltpu.VMEM((2 * length, channels), F32),
            pltpu.VMEM((channels, channels), BF16),
            pltpu.VMEM((channels, channels), BF16),
        ],
        compiler_params=params(48),
        name="attend",
    )(up, stats, norm_gain.reshape(1, channels), block, qkv_weight, out_weight)


def unpack_kernel(block_ref, out_ref, wide):
    devices, share, _, part, _ = block_ref.shape
    frames, pixels, _ = out_ref.shape
    for half in range(wide.shape[0]):
        lanes = slice(half * LANES, (half + 1) * LANES)
        for s in range(devices):
            for j in range(share):
                for parity in range(2):
                    start = parity * pixels + s * share + j
                    rows = block_ref[s, j, parity, :, lanes].astype(F32)
                    wide[half, pl.ds(start, part, stride=2 * pixels), :] = rows
        for f in range(frames):
            out_ref[f, :, lanes] = wide[half, f * pixels : (f + 1) * pixels, :].astype(BF16)


def unpack(block):
    devices, share, _, part, channels = block.shape
    frames, pixels = 2 * part, devices * share
    return pl.pallas_call(
        unpack_kernel,
        out_shape=jax.ShapeDtypeStruct((frames, pixels, channels), BF16),
        scratch_shapes=[pltpu.VMEM((channels // LANES, frames * pixels, LANES), F32)],
        compiler_params=params(24),
        name="unpack_output",
    )(block)


def per_device(latent, conv_weight, norm_gain, frame_embed, qkv_weight, out_weight):
    devices = lax.axis_size("frames")
    everyone = devices * lax.axis_size("rows")
    share = latent.shape[1] // devices
    sent = pack(latent, frame_embed, devices)
    block = lax.all_to_all(sent, "frames", 0, 0)
    up, stats = upsample(block, conv_weight, share)
    stats = lax.all_to_all(
        jnp.broadcast_to(stats[None], (everyone,) + stats.shape), ("rows", "frames"), 0, 0
    )
    blended = attend(up, stats, norm_gain, block, qkv_weight, out_weight)
    return unpack(lax.all_to_all(blended, "frames", 0, 0))


def solution(mesh):
    return jax.shard_map(
        per_device,
        mesh=mesh,
        in_specs=(P("frames", "rows", None), P(), P(), P("frames", None), P(), P()),
        out_specs=P("frames", "rows", None),
        check_vma=False,
    )
```

```python
import functools

import jax
import jax.numpy as jnp
from jax import lax
from jax.experimental import pallas as pl
from jax.experimental.pallas import tpu as pltpu
from jax.sharding import PartitionSpec as P

HEAD_DIM = 64
GROUPS = 32
EPSILON = 1e-06
LANES = 128
LOG2E = 1.4426950408889634
HIGHEST = lax.Precision.HIGHEST
BF16 = jnp.bfloat16
F32 = jnp.float32
NT = (((1,), (1,)), ((), ()))


def params(mib):
    return pltpu.CompilerParams(vmem_limit_bytes=mib * 1024 * 1024)


def pack_kernel(latent_ref, embed_ref, out_ref, wide, embed_wide):
    frames, pixels, _ = latent_ref.shape
    devices = out_ref.shape[0]
    share = pixels // devices
    for half in range(wide.shape[0]):
        lanes = slice(half * LANES, (half + 1) * LANES)
        for f in range(frames):
            wide[half, f * pixels : (f + 1) * pixels, :] = latent_ref[f, :, lanes].astype(F32)
        embed_wide[half] = embed_ref[:, lanes].astype(F32)
        for p in range(pixels):
            d, j = divmod(p, share)
            rows = wide[half, pl.ds(p, frames, stride=pixels), :].astype(BF16)
            out_ref[d, j * frames : (j + 1) * frames, lanes] = rows
        for parity in range(2):
            rows = embed_wide[half, pl.ds(parity, frames, stride=2), :].astype(BF16)
            base = share * frames + parity * frames
            for d in range(devices):
                out_ref[d, base : base + frames, lanes] = rows


def pack(latent, frame_embed, devices):
    frames, pixels, channels = latent.shape
    rows = pixels // devices * frames + 2 * frames
    return pl.pallas_call(
        pack_kernel,
        out_shape=jax.ShapeDtypeStruct((devices, rows, channels), BF16),
        scratch_shapes=[
            pltpu.VMEM((channels // LANES, frames * pixels, LANES), F32),
            pltpu.VMEM((channels // LANES, 2 * frames, LANES), F32),
        ],
        compiler_params=params(24),
        name="pack_latent",
    )(latent, frame_embed)


def group_matrix(channels, offset):
    size = channels // GROUPS
    channel = lax.broadcasted_iota(jnp.int32, (channels, LANES), 0)
    lane = lax.broadcasted_iota(jnp.int32, (channels, LANES), 1)
    return jnp.where(channel // size + offset == lane, 1.0, 0.0).astype(F32)


def group_spread(channels):
    size = channels // GROUPS
    lane = lax.broadcasted_iota(jnp.int32, (LANES, channels), 0)
    channel = lax.broadcasted_iota(jnp.int32, (LANES, channels), 1)
    return jnp.where(channel // size == lane, 1.0, 0.0).astype(F32)


def exact_dot(a, b):
    return jnp.dot(a, b, precision=HIGHEST, preferred_element_type=F32)


def upsample_kernel(share, block_ref, conv_ref, up_ref, stats_ref, taps):
    devices = block_ref.shape[0]
    channels = block_ref.shape[2]
    part = (block_ref.shape[1]) // (share + 2)
    length = devices * part
    row = lax.broadcasted_iota(jnp.int32, (length, channels), 0)
    for j in range(share):
        here = jnp.concatenate([block_ref[s, j * part : (j + 1) * part, :] for s in range(devices)], axis=0)
        wide = here.astype(F32)
        before = jnp.where(row == 0, 0.0, pltpu.roll(wide, 1, 0))
        after = jnp.where(row == length - 1, 0.0, pltpu.roll(wide, length - 1, 0))
        rows = slice(j * length, (j + 1) * length)
        taps[0, rows, :] = before.astype(BF16)
        taps[1, rows, :] = here
        taps[2, rows, :] = after.astype(BF16)

    def tap(source, index):
        return jnp.dot(taps[source], conv_ref[index], preferred_element_type=F32)

    even = (tap(1, 1) + tap(0, 3)).astype(BF16)
    odd = (tap(2, 0) + tap(1, 2)).astype(BF16)
    for j in range(share):
        up_ref[j, 0] = even[j * length : (j + 1) * length]
        up_ref[j, 1] = odd[j * length : (j + 1) * length]
    count = share * 2 * length * (channels // GROUPS)
    total = jnp.zeros((8, channels), F32)

    def add_rows(i, total):
        chunk = up_ref[i].astype(F32).reshape(-1, 8, channels)
        return total + jnp.sum(chunk, axis=0)

    total = lax.fori_loop(0, share, add_rows, total)
    total = jnp.broadcast_to(jnp.sum(total, axis=0, keepdims=True), (8, channels))
    mean = exact_dot(total, group_matrix(channels, 0)) / count
    center = exact_dot(mean, group_spread(channels))[0:1]

    def add_squares(i, spread):
        away = (up_ref[i].astype(F32).reshape(-1, channels) - center).reshape(-1, 8, channels)
        return spread + jnp.sum(away * away, axis=0)

    spread = lax.fori_loop(0, share, add_squares, jnp.zeros((8, channels), F32))
    spread = jnp.broadcast_to(jnp.sum(spread, axis=0, keepdims=True), (8, channels))
    stats_ref[...] = (mean + exact_dot(spread, group_matrix(channels, LANES // 2)))[0:1]


def upsample(block, conv_weight, share):
    devices, rows, channels = block.shape
    length = devices * (rows // (share + 2))
    return pl.pallas_call(
        functools.partial(upsample_kernel, share),
        out_shape=(
            jax.ShapeDtypeStruct((share, 2, length, channels), BF16),
            jax.ShapeDtypeStruct((1, LANES), F32),
        ),
        scratch_shapes=[pltpu.VMEM((3, share * length, channels), BF16)],
        compiler_params=params(48),
        name="upsample",
    )(block, conv_weight)


def moments(stats, count, gain):
    channels = gain.shape[1]
    holders = stats.shape[0]
    center = jnp.sum(stats, axis=0, keepdims=True) / holders
    away = stats - center
    between = jnp.sum(away * away, axis=0, keepdims=True) * count
    within = pltpu.roll(center, LANES // 2, 1) * holders
    lane = lax.broadcasted_iota(jnp.int32, (1, LANES), 1)
    variance = jnp.where(lane < GROUPS, (between + within) / (count * holders), 0.0)
    center = jnp.where(lane < GROUPS, center, 0.0)
    both = jnp.concatenate(
        [jnp.broadcast_to(center, (8, LANES)), jnp.broadcast_to(variance, (8, LANES))], axis=0
    )
    both = exact_dot(both, group_spread(channels))
    return both[0:1], lax.rsqrt(both[8:9] + EPSILON) * gain.astype(F32)


def attend_pixel(qkv):
    rows, channels = qkv.shape[0], qkv.shape[1] // 3
    heads = channels // HEAD_DIM
    head = lax.broadcasted_iota(jnp.int32, (rows, channels), 1) // HEAD_DIM
    first = lax.broadcasted_iota(jnp.int32, (rows, LANES), 1) < HEAD_DIM
    queries, keys, values = (qkv[:, i * channels : (i + 1) * channels] for i in range(3))
    zeros = jnp.zeros_like(queries)
    stacked = jnp.concatenate([jnp.where(head == h, queries, zeros) for h in range(heads)], axis=0)
    scores = lax.dot_general(stacked, keys, NT, preferred_element_type=F32)
    ones = jnp.ones((rows, LANES), BF16)
    context = []
    for pair in range(heads // 2):
        part = scores[pair * 2 * rows : (pair + 1) * 2 * rows]
        top = jnp.max(part, axis=1, keepdims=True)
        weights = jnp.exp2((part - top) * (LOG2E * HEAD_DIM**-0.5)).astype(BF16)
        value = jnp.concatenate([values[:, pair * LANES : (pair + 1) * LANES], ones], axis=1)
        sums = jnp.dot(weights, value, preferred_element_type=F32)
        above, total = (
            jnp.where(first, sums[:rows, i * LANES : (i + 1) * LANES], sums[rows:, i * LANES : (i + 1) * LANES])
            for i in range(2)
        )
        context.append((above * (1.0 / total)).astype(BF16))
    return jnp.concatenate(context, axis=1)


def attend_kernel(
    count, batch, up_ref, stats_ref, gain_ref, block_ref, qkv_ref, out_weight_ref, out_ref, embed, projected, context
):
    share, _, length, channels = up_ref.shape
    devices = block_ref.shape[0]
    part = length // devices
    frames = 2 * length
    center, scale = moments(stats_ref[...].reshape(-1, LANES), count, gain_ref[...])
    base = share * part
    for parity in range(2):
        for s in range(devices):
            start = base + parity * part
            embed[parity * length + s * part : parity * length + (s + 1) * part, :] = block_ref[
                s, start : start + part, :
            ].astype(F32)

    def project(first, pixels):
        up = up_ref[pl.ds(first, pixels)].reshape(pixels, frames, channels).astype(F32)
        normed = ((up - center) * scale + embed[...]).astype(BF16).reshape(pixels * frames, channels)
        rows = pl.ds(pl.multiple_of(first * frames, frames), pixels * frames)
        projected[rows, :] = jnp.dot(normed, qkv_ref[...], preferred_element_type=F32).astype(BF16)

    def project_batch(i, carry):
        project(i * batch, batch)
        return carry

    lax.fori_loop(0, share // batch, project_batch, 0)
    if share % batch:
        project(share - share % batch, share % batch)
    for j in range(share):
        rows = slice(j * frames, (j + 1) * frames)
        context[rows, :] = attend_pixel(projected[rows, :])
    mixed = jnp.dot(context[...], out_weight_ref[...], preferred_element_type=F32)
    for j in range(share):
        up = up_ref[j].reshape(frames, channels).astype(F32)
        blended = (up + mixed[j * frames : (j + 1) * frames]).astype(BF16)
        for d in range(devices):
            for parity in range(2):
                start = parity * length + d * part
                out_ref[d, j, parity] = blended[start : start + part]


def attend(up, stats, norm_gain, block, qkv_weight, out_weight):
    share, _, length, channels = up.shape
    devices = block.shape[0]
    part = length // devices
    count = share * 2 * length * (channels // GROUPS)
    rows = share * 2 * length
    return pl.pallas_call(
        functools.partial(attend_kernel, count, 4),
        out_shape=jax.ShapeDtypeStruct((devices, share, 2, part, channels), BF16),
        scratch_shapes=[
            pltpu.VMEM((2 * length, channels), F32),
            pltpu.VMEM((rows, 3 * channels), BF16),
            pltpu.VMEM((rows, channels), BF16),
        ],
        compiler_params=params(48),
        name="attend",
    )(up, stats, norm_gain.reshape(1, channels), block, qkv_weight, out_weight)


def unpack_kernel(block_ref, out_ref, wide):
    devices, share, _, part, _ = block_ref.shape
    frames, pixels, _ = out_ref.shape
    for half in range(wide.shape[0]):
        lanes = slice(half * LANES, (half + 1) * LANES)
        for s in range(devices):
            for j in range(share):
                for parity in range(2):
                    start = parity * pixels + s * share + j
                    rows = block_ref[s, j, parity, :, lanes].astype(F32)
                    wide[half, pl.ds(start, part, stride=2 * pixels), :] = rows
        for f in range(frames):
            out_ref[f, :, lanes] = wide[half, f * pixels : (f + 1) * pixels, :].astype(BF16)


def unpack(block):
    devices, share, _, part, channels = block.shape
    frames, pixels = 2 * part, devices * share
    return pl.pallas_call(
        unpack_kernel,
        out_shape=jax.ShapeDtypeStruct((frames, pixels, channels), BF16),
        scratch_shapes=[pltpu.VMEM((channels // LANES, frames * pixels, LANES), F32)],
        compiler_params=params(24),
        name="unpack_output",
    )(block)


def per_device(latent, conv_weight, norm_gain, frame_embed, qkv_weight, out_weight):
    devices = lax.axis_size("frames")
    everyone = devices * lax.axis_size("rows")
    share = latent.shape[1] // devices
    sent = pack(latent, frame_embed, devices)
    block = lax.all_to_all(sent, "frames", 0, 0)
    up, stats = upsample(block, conv_weight, share)
    stats = lax.all_to_all(
        jnp.broadcast_to(stats[None], (everyone,) + stats.shape), ("rows", "frames"), 0, 0
    )
    blended = attend(up, stats, norm_gain, block, qkv_weight, out_weight)
    return unpack(lax.all_to_all(blended, "frames", 0, 0))


def solution(mesh):
    return jax.shard_map(
        per_device,
        mesh=mesh,
        in_specs=(P("frames", "rows", None), P(), P(), P("frames", None), P(), P()),
        out_specs=P("frames", "rows", None),
        check_vma=False,
    )
```

```python
import functools

import jax
import jax.numpy as jnp
from jax import lax
from jax.experimental import pallas as pl
from jax.experimental.pallas import tpu as pltpu
from jax.sharding import PartitionSpec as P

HEAD_DIM = 64
GROUPS = 32
EPSILON = 1e-06
LANES = 128
LOG2E = 1.4426950408889634
HIGHEST = lax.Precision.HIGHEST
BF16 = jnp.bfloat16
F32 = jnp.float32
NT = (((1,), (1,)), ((), ()))


def params(mib):
    return pltpu.CompilerParams(vmem_limit_bytes=mib * 1024 * 1024)


def pack_kernel(latent_ref, embed_ref, out_ref, wide, embed_wide):
    frames, pixels, _ = latent_ref.shape
    devices = out_ref.shape[0]
    share = pixels // devices
    for half in range(wide.shape[0]):
        lanes = slice(half * LANES, (half + 1) * LANES)
        for f in range(frames):
            wide[half, f * pixels : (f + 1) * pixels, :] = latent_ref[f, :, lanes].astype(F32)
        embed_wide[half] = embed_ref[:, lanes].astype(F32)
        for p in range(pixels):
            d, j = divmod(p, share)
            rows = wide[half, pl.ds(p, frames, stride=pixels), :].astype(BF16)
            out_ref[d, j * frames : (j + 1) * frames, lanes] = rows
        for parity in range(2):
            rows = embed_wide[half, pl.ds(parity, frames, stride=2), :].astype(BF16)
            base = share * frames + parity * frames
            for d in range(devices):
                out_ref[d, base : base + frames, lanes] = rows


def pack(latent, frame_embed, devices):
    frames, pixels, channels = latent.shape
    rows = pixels // devices * frames + 2 * frames
    return pl.pallas_call(
        pack_kernel,
        out_shape=jax.ShapeDtypeStruct((devices, rows, channels), BF16),
        scratch_shapes=[
            pltpu.VMEM((channels // LANES, frames * pixels, LANES), F32),
            pltpu.VMEM((channels // LANES, 2 * frames, LANES), F32),
        ],
        compiler_params=params(24),
        name="pack_latent",
    )(latent, frame_embed)


def group_matrix(channels, offset):
    size = channels // GROUPS
    channel = lax.broadcasted_iota(jnp.int32, (channels, LANES), 0)
    lane = lax.broadcasted_iota(jnp.int32, (channels, LANES), 1)
    return jnp.where(channel // size + offset == lane, 1.0, 0.0).astype(F32)


def group_spread(channels):
    size = channels // GROUPS
    lane = lax.broadcasted_iota(jnp.int32, (LANES, channels), 0)
    channel = lax.broadcasted_iota(jnp.int32, (LANES, channels), 1)
    return jnp.where(channel // size == lane, 1.0, 0.0).astype(F32)


def exact_dot(a, b):
    return jnp.dot(a, b, precision=HIGHEST, preferred_element_type=F32)


def upsample_kernel(share, block_ref, conv_ref, up_ref, stats_ref, taps):
    devices = block_ref.shape[0]
    channels = block_ref.shape[2]
    part = (block_ref.shape[1]) // (share + 2)
    length = devices * part
    row = lax.broadcasted_iota(jnp.int32, (length, channels), 0)
    for j in range(share):
        here = jnp.concatenate([block_ref[s, j * part : (j + 1) * part, :] for s in range(devices)], axis=0)
        wide = here.astype(F32)
        before = jnp.where(row == 0, 0.0, pltpu.roll(wide, 1, 0))
        after = jnp.where(row == length - 1, 0.0, pltpu.roll(wide, length - 1, 0))
        rows = slice(j * length, (j + 1) * length)
        taps[0, rows, :] = before.astype(BF16)
        taps[1, rows, :] = here
        taps[2, rows, :] = after.astype(BF16)

    def tap(source, index):
        return jnp.dot(taps[source], conv_ref[index], preferred_element_type=F32)

    even = (tap(1, 1) + tap(0, 3)).astype(BF16)
    odd = (tap(2, 0) + tap(1, 2)).astype(BF16)
    count = share * 2 * length * (channels // GROUPS)
    fold = 32

    def column_sums(pieces):
        total = sum(jnp.sum(piece.reshape(-1, fold, channels), axis=0) for piece in pieces)
        return jnp.broadcast_to(jnp.sum(total, axis=0, keepdims=True), (8, channels))

    pivot = column_sums([frames[0:length].astype(F32) for frames in (even, odd)])
    pivot = exact_dot(pivot, group_matrix(channels, 0)) * (share / count)
    center = exact_dot(pivot, group_spread(channels))[0:1]
    shifts = jnp.zeros((fold, channels), F32)
    squares = jnp.zeros((fold, channels), F32)
    for j in range(share):
        for parity, frames in enumerate((even, odd)):
            piece = frames[j * length : (j + 1) * length]
            up_ref[j, parity] = piece
            away = piece.astype(F32) - center
            shifts += jnp.sum(away.reshape(-1, fold, channels), axis=0)
            squares += jnp.sum((away * away).reshape(-1, fold, channels), axis=0)
    sums = jnp.concatenate([column_sums([shifts]), column_sums([squares])], axis=0)
    sums = exact_dot(sums, group_matrix(channels, 0))
    shift, square = sums[0:1], sums[8:9]
    own = pivot[0:1] + shift / count + pltpu.roll(square - shift * shift / count, LANES // 2, 1)
    stats_ref[...] = jnp.broadcast_to(own, stats_ref.shape)


def upsample(block, conv_weight, share, copies):
    devices, rows, channels = block.shape
    length = devices * (rows // (share + 2))
    return pl.pallas_call(
        functools.partial(upsample_kernel, share),
        out_shape=(
            jax.ShapeDtypeStruct((share, 2, length, channels), BF16),
            jax.ShapeDtypeStruct((copies, LANES), F32),
        ),
        scratch_shapes=[pltpu.VMEM((3, share * length, channels), BF16)],
        compiler_params=params(48),
        name="upsample",
    )(block, conv_weight)


def moments(stats, count, gain):
    channels = gain.shape[1]
    holders = stats.shape[0]
    center = jnp.sum(stats, axis=0, keepdims=True) / holders
    away = stats - center
    between = jnp.sum(away * away, axis=0, keepdims=True) * count
    within = pltpu.roll(center, LANES // 2, 1) * holders
    lane = lax.broadcasted_iota(jnp.int32, (1, LANES), 1)
    variance = jnp.where(lane < GROUPS, (between + within) / (count * holders), 0.0)
    center = jnp.where(lane < GROUPS, center, 0.0)
    both = jnp.concatenate(
        [jnp.broadcast_to(center, (8, LANES)), jnp.broadcast_to(variance, (8, LANES))], axis=0
    )
    both = exact_dot(both, group_spread(channels))
    return both[0:1], lax.rsqrt(both[8:9] + EPSILON) * gain.astype(F32)


def attend_pixel(queries, keys, values):
    rows, channels = queries.shape
    heads = channels // HEAD_DIM
    head = lax.broadcasted_iota(jnp.int32, (rows, channels), 1) // HEAD_DIM
    first = lax.broadcasted_iota(jnp.int32, (rows, LANES), 1) < HEAD_DIM
    zeros = jnp.zeros_like(queries)
    stacked = jnp.concatenate([jnp.where(head == h, queries, zeros) for h in range(heads)], axis=0)
    scores = lax.dot_general(stacked, keys, NT, preferred_element_type=F32)
    ones = jnp.ones((keys.shape[0], LANES), BF16)
    context = []
    for pair in range(heads // 2):
        part = scores[pair * 2 * rows : (pair + 1) * 2 * rows]
        top = jnp.max(part, axis=1, keepdims=True)
        weights = jnp.exp2((part - top) * (LOG2E * HEAD_DIM**-0.5)).astype(BF16)
        value = jnp.concatenate([values[:, pair * LANES : (pair + 1) * LANES], ones], axis=1)
        sums = jnp.dot(weights, value, preferred_element_type=F32)
        above, total = (
            jnp.where(first, sums[:rows, i * LANES : (i + 1) * LANES], sums[rows:, i * LANES : (i + 1) * LANES])
            for i in range(2)
        )
        context.append((above * (1.0 / total)).astype(BF16))
    return jnp.concatenate(context, axis=1)


def attend_targets(steps, up_ref, projected, out_weight_ref, out_refs, context):
    share, _, length, channels = up_ref.shape
    part = out_refs[0].shape[2]
    me = lax.axis_index("frames")
    starts = [
        pl.multiple_of(parity * length + (me ^ k) * part, part) for k in steps for parity in range(2)
    ]
    rows = len(starts) * part
    for j in range(share):
        base = j * 2 * length
        queries = jnp.concatenate([projected[pl.ds(base + s, part), 0:channels] for s in starts], axis=0)
        keys = projected[base : base + 2 * length, channels : 2 * channels]
        values = projected[base : base + 2 * length, 2 * channels : 3 * channels]
        context[j * rows : (j + 1) * rows, :] = attend_pixel(queries, keys, values)
    mixed = jnp.dot(context[0 : share * rows, :], out_weight_ref[...], preferred_element_type=F32)
    for j in range(share):
        for i, k in enumerate(steps):
            for parity in range(2):
                place = 2 * i + parity
                start = pl.multiple_of((me ^ k) * part, part)
                up = up_ref[j, parity, pl.ds(start, part), :].astype(F32)
                first = j * rows + place * part
                out_refs[i][j, parity] = (up + mixed[first : first + part]).astype(BF16)


def attend_first_kernel(
    steps, count, batch, up_ref, stats_ref, gain_ref, block_ref, qkv_ref, out_weight_ref, *refs
):
    *out_refs, projected, embed, context = refs
    share, _, length, channels = up_ref.shape
    devices = block_ref.shape[0]
    part = length // devices
    frames = 2 * length
    center, scale = moments(stats_ref[...], count, gain_ref[...])
    base = share * part
    for parity in range(2):
        for s in range(devices):
            start = base + parity * part
            embed[parity * length + s * part : parity * length + (s + 1) * part, :] = block_ref[
                s, start : start + part, :
            ].astype(F32)

    def project(first, pixels):
        up = up_ref[pl.ds(first, pixels)].reshape(pixels, frames, channels).astype(F32)
        normed = ((up - center) * scale + embed[...]).astype(BF16).reshape(pixels * frames, channels)
        rows = pl.ds(pl.multiple_of(first * frames, frames), pixels * frames)
        projected[rows, :] = jnp.dot(normed, qkv_ref[...], preferred_element_type=F32).astype(BF16)

    def project_batch(i, carry):
        project(i * batch, batch)
        return carry

    lax.fori_loop(0, share // batch, project_batch, 0)
    if share % batch:
        project(share - share % batch, share % batch)
    attend_targets(steps, up_ref, projected, out_weight_ref, out_refs, context)


def attend_rest_kernel(steps, up_ref, projected, out_weight_ref, *refs):
    *out_refs, context = refs
    attend_targets(steps, up_ref, projected, out_weight_ref, out_refs, context)


def attend_cost(share, length, channels, steps, part):
    rows = share * 2 * part * steps
    flops = 2 * rows * channels * (2 * length * 8 + channels)
    return pl.CostEstimate(flops=flops, bytes_accessed=rows * channels * 4, transcendentals=rows * 8 * length)


def attend_first(steps, up, stats, norm_gain, block, qkv_weight, out_weight):
    share, _, length, channels = up.shape
    devices = block.shape[0]
    part = length // devices
    count = share * 2 * length * (channels // GROUPS)
    rows = share * 2 * length
    piece = jax.ShapeDtypeStruct((share, 2, part, channels), BF16)
    return pl.pallas_call(
        functools.partial(attend_first_kernel, steps, count, 4),
        out_shape=(piece,) * len(steps) + (jax.ShapeDtypeStruct((rows, 3 * channels), BF16),),
        scratch_shapes=[
            pltpu.VMEM((2 * length, channels), F32),
            pltpu.VMEM((share * 2 * part * len(steps), channels), BF16),
        ],
        compiler_params=params(40),
        cost_estimate=attend_cost(share, length, channels, len(steps), part),
        name="attend_first",
    )(up, stats, norm_gain.reshape(1, channels), block, qkv_weight, out_weight)


def attend_rest(steps, up, projected, out_weight, part):
    share, _, length, channels = up.shape
    piece = jax.ShapeDtypeStruct((share, 2, part, channels), BF16)
    return pl.pallas_call(
        functools.partial(attend_rest_kernel, steps),
        out_shape=(piece,) * len(steps),
        scratch_shapes=[pltpu.VMEM((share * 2 * part * len(steps), channels), BF16)],
        compiler_params=params(40),
        cost_estimate=attend_cost(share, length, channels, len(steps), part),
        name="attend_rest",
    )(up, projected, out_weight)


def unpack_kernel(steps, *refs):
    *block_refs, out_hbm, held, wide, sems = refs
    frames, pixels, _ = held.shape
    pieces = sems.shape[1]
    step = frames // pieces
    copies = []
    share, _, part, _ = block_refs[0].shape
    me = lax.axis_index("frames")
    for half in range(wide.shape[0]):
        lanes = slice(half * LANES, (half + 1) * LANES)
        for k, block_ref in zip(steps, block_refs):
            for j in range(share):
                for parity in range(2):
                    start = parity * pixels + j + (me ^ k) * share
                    rows = block_ref[j, parity, :, lanes].astype(F32)
                    wide[half, pl.ds(start, part, stride=2 * pixels), :] = rows
        for i in range(pieces):
            for f in range(i * step, (i + 1) * step):
                held[f, :, lanes] = wide[half, f * pixels : (f + 1) * pixels, :].astype(BF16)
            span = (pl.ds(i * step, step), slice(None), pl.ds(half * LANES, LANES))
            copies.append(pltpu.make_async_copy(held.at[span], out_hbm.at[span], sems.at[half, i]))
            copies[-1].start()
    for copy in copies:
        copy.wait()


def unpack(steps, blocks):
    share, _, part, channels = blocks[0].shape
    frames, pixels = 2 * part, len(blocks) * share
    return pl.pallas_call(
        functools.partial(unpack_kernel, steps),
        out_shape=jax.ShapeDtypeStruct((frames, pixels, channels), BF16),
        out_specs=pl.BlockSpec(memory_space=pltpu.HBM),
        scratch_shapes=[
            pltpu.VMEM((frames, pixels, channels), BF16),
            pltpu.VMEM((channels // LANES, frames * pixels, LANES), F32),
            pltpu.SemaphoreType.DMA((channels // LANES, 4)),
        ],
        compiler_params=params(24),
        name="unpack_output",
    )(*blocks)


TARGETS = ((4, 2), (6, 7, 5), (1, 3, 0))


def per_device(latent, conv_weight, norm_gain, frame_embed, qkv_weight, out_weight):
    devices = lax.axis_size("frames")
    everyone = devices * lax.axis_size("rows")
    share = latent.shape[1] // devices
    sent = pack(latent, frame_embed, devices)
    block = lax.all_to_all(sent, "frames", 0, 0)
    up, copies = upsample(block, conv_weight, share, everyone)
    stats = lax.all_to_all(copies, ("rows", "frames"), 0, 0)

    def send(piece, k):
        return lax.ppermute(piece, "frames", [(i, i ^ k) for i in range(devices)]) if k else piece

    *pieces, projected = attend_first(TARGETS[0], up, stats, norm_gain, block, qkv_weight, out_weight)
    got = [send(piece, k) for piece, k in zip(pieces, TARGETS[0])]
    for steps in TARGETS[1:]:
        pieces = attend_rest(steps, up, projected, out_weight, pieces[0].shape[2])
        got += [send(piece, k) for piece, k in zip(pieces, steps)]
    return unpack(sum(TARGETS, ()), got)


def solution(mesh):
    return jax.shard_map(
        per_device,
        mesh=mesh,
        in_specs=(P("frames", "rows", None), P(), P(), P("frames", None), P(), P()),
        out_specs=P("frames", "rows", None),
        check_vma=False,
    )
```

```python
import functools

import jax
import jax.numpy as jnp
from jax import lax
from jax.experimental import pallas as pl
from jax.experimental.pallas import tpu as pltpu
from jax.sharding import PartitionSpec as P

HEAD_DIM = 64
GROUPS = 32
EPSILON = 1e-06
LANES = 128
LOG2E = 1.4426950408889634
HIGHEST = lax.Precision.HIGHEST
BF16 = jnp.bfloat16
F32 = jnp.float32
NT = (((1,), (1,)), ((), ()))


def params(mib):
    return pltpu.CompilerParams(vmem_limit_bytes=mib * 1024 * 1024)


def pack_kernel(latent_ref, embed_ref, out_ref, wide, embed_wide):
    frames, pixels, _ = latent_ref.shape
    devices = out_ref.shape[0]
    share = pixels // devices
    for half in range(wide.shape[0]):
        lanes = slice(half * LANES, (half + 1) * LANES)
        for f in range(frames):
            wide[half, f * pixels : (f + 1) * pixels, :] = latent_ref[f, :, lanes].astype(F32)
        embed_wide[half] = embed_ref[:, lanes].astype(F32)
        for p in range(pixels):
            d, j = divmod(p, share)
            rows = wide[half, pl.ds(p, frames, stride=pixels), :].astype(BF16)
            out_ref[d, j * frames : (j + 1) * frames, lanes] = rows
        for parity in range(2):
            rows = embed_wide[half, pl.ds(parity, frames, stride=2), :].astype(BF16)
            base = share * frames + parity * frames
            for d in range(devices):
                out_ref[d, base : base + frames, lanes] = rows


def pack(latent, frame_embed, devices):
    frames, pixels, channels = latent.shape
    rows = pixels // devices * frames + 2 * frames
    return pl.pallas_call(
        pack_kernel,
        out_shape=jax.ShapeDtypeStruct((devices, rows, channels), BF16),
        scratch_shapes=[
            pltpu.VMEM((channels // LANES, frames * pixels, LANES), F32),
            pltpu.VMEM((channels // LANES, 2 * frames, LANES), F32),
        ],
        compiler_params=params(24),
        name="pack_latent",
    )(latent, frame_embed)


def group_matrix(channels, offset):
    size = channels // GROUPS
    channel = lax.broadcasted_iota(jnp.int32, (channels, LANES), 0)
    lane = lax.broadcasted_iota(jnp.int32, (channels, LANES), 1)
    return jnp.where(channel // size + offset == lane, 1.0, 0.0).astype(F32)


def group_spread(channels):
    size = channels // GROUPS
    lane = lax.broadcasted_iota(jnp.int32, (LANES, channels), 0)
    channel = lax.broadcasted_iota(jnp.int32, (LANES, channels), 1)
    return jnp.where(channel // size == lane, 1.0, 0.0).astype(F32)


def exact_dot(a, b):
    return jnp.dot(a, b, precision=HIGHEST, preferred_element_type=F32)


def upsample_kernel(share, block_ref, conv_ref, up_ref, stats_ref, taps):
    devices = block_ref.shape[0]
    channels = block_ref.shape[2]
    part = (block_ref.shape[1]) // (share + 2)
    length = devices * part
    row = lax.broadcasted_iota(jnp.int32, (length, channels), 0)
    for j in range(share):
        here = jnp.concatenate([block_ref[s, j * part : (j + 1) * part, :] for s in range(devices)], axis=0)
        wide = here.astype(F32)
        before = jnp.where(row == 0, 0.0, pltpu.roll(wide, 1, 0))
        after = jnp.where(row == length - 1, 0.0, pltpu.roll(wide, length - 1, 0))
        rows = slice(j * length, (j + 1) * length)
        taps[0, rows, :] = before.astype(BF16)
        taps[1, rows, :] = here
        taps[2, rows, :] = after.astype(BF16)

    count = share * 2 * length * (channels // GROUPS)
    fold = 16

    def column_sums(pieces):
        total = sum(jnp.sum(piece.reshape(-1, fold, channels), axis=0) for piece in pieces)
        return jnp.broadcast_to(jnp.sum(total, axis=0, keepdims=True), (8, channels))

    shifts = jnp.zeros((fold, channels), F32)
    squares = jnp.zeros((fold, channels), F32)
    first = 0
    for pixels in (1, 6, 6):
        rows = slice(first * length, (first + pixels) * length)

        def tap(source, index):
            return jnp.dot(taps[source, rows, :], conv_ref[index], preferred_element_type=F32)

        even = (tap(1, 1) + tap(0, 3)).astype(BF16)
        odd = (tap(2, 0) + tap(1, 2)).astype(BF16)
        if first == 0:
            pivot = column_sums([frames[0:length].astype(F32) for frames in (even, odd)])
            pivot = exact_dot(pivot, group_matrix(channels, 0)) * (share / count)
            center = exact_dot(pivot, group_spread(channels))[0:1]
        for j in range(pixels):
            for parity, frames in enumerate((even, odd)):
                piece = frames[j * length : (j + 1) * length]
                up_ref[first + j, parity] = piece
                away = piece.astype(F32) - center
                shifts += jnp.sum(away.reshape(-1, fold, channels), axis=0)
                squares += jnp.sum((away * away).reshape(-1, fold, channels), axis=0)
        first += pixels
    sums = jnp.concatenate([column_sums([shifts]), column_sums([squares])], axis=0)
    sums = exact_dot(sums, group_matrix(channels, 0))
    shift, square = sums[0:1], sums[8:9]
    own = pivot[0:1] + shift / count + pltpu.roll(square - shift * shift / count, LANES // 2, 1)
    stats_ref[...] = jnp.broadcast_to(own, stats_ref.shape)


def upsample(block, conv_weight, share, copies):
    devices, rows, channels = block.shape
    length = devices * (rows // (share + 2))
    return pl.pallas_call(
        functools.partial(upsample_kernel, share),
        out_shape=(
            jax.ShapeDtypeStruct((share, 2, length, channels), BF16),
            jax.ShapeDtypeStruct((copies, LANES), F32),
        ),
        scratch_shapes=[pltpu.VMEM((3, share * length, channels), BF16)],
        compiler_params=params(48),
        name="upsample",
    )(block, conv_weight)


def moments(stats, count, gain):
    channels = gain.shape[1]
    holders = stats.shape[0]
    center = jnp.sum(stats, axis=0, keepdims=True) / holders
    away = stats - center
    between = jnp.sum(away * away, axis=0, keepdims=True) * count
    within = pltpu.roll(center, LANES // 2, 1) * holders
    lane = lax.broadcasted_iota(jnp.int32, (1, LANES), 1)
    variance = jnp.where(lane < GROUPS, (between + within) / (count * holders), 0.0)
    center = jnp.where(lane < GROUPS, center, 0.0)
    both = jnp.concatenate(
        [jnp.broadcast_to(center, (8, LANES)), jnp.broadcast_to(variance, (8, LANES))], axis=0
    )
    both = exact_dot(both, group_spread(channels))
    return both[0:1], lax.rsqrt(both[8:9] + EPSILON) * gain.astype(F32)


def attend_pixel(queries, keys, values):
    rows, channels = queries.shape
    heads = channels // HEAD_DIM
    head = lax.broadcasted_iota(jnp.int32, (rows, channels), 1) // HEAD_DIM
    first = lax.broadcasted_iota(jnp.int32, (rows, LANES), 1) < HEAD_DIM
    zeros = jnp.zeros_like(queries)
    stacked = jnp.concatenate([jnp.where(head == h, queries, zeros) for h in range(heads)], axis=0)
    scores = lax.dot_general(stacked, keys, NT, preferred_element_type=F32)
    top = jnp.max(scores, axis=1, keepdims=True)
    weights = jnp.exp2((scores - top) * (LOG2E * HEAD_DIM**-0.5))
    scale = 1.0 / jnp.sum(weights, axis=1, keepdims=True)
    mixed = jnp.dot(weights.astype(BF16), values, preferred_element_type=F32)
    context = []
    for pair in range(heads // 2):
        lanes = slice(pair * LANES, (pair + 1) * LANES)
        upper, lower = (slice((2 * pair + i) * rows, (2 * pair + i + 1) * rows) for i in range(2))
        part = jnp.where(first, mixed[upper, lanes], mixed[lower, lanes])
        context.append((part * jnp.where(first, scale[upper], scale[lower])).astype(BF16))
    return jnp.concatenate(context, axis=1)


def attend_targets(steps, up_ref, normed, keyed, qkv_ref, out_weight_ref, out_refs, queries, context):
    share, _, length, channels = up_ref.shape
    part = out_refs[0].shape[2]
    me = lax.axis_index("frames")
    starts = [
        pl.multiple_of(parity * length + (me ^ k) * part, part) for k in steps for parity in range(2)
    ]
    rows = len(starts) * part
    for j in range(share):
        for i, start in enumerate(starts):
            first = j * rows + i * part
            queries[first : first + part, :] = normed[pl.ds(j * 2 * length + start, part), :]
    queries[...] = jnp.dot(queries[...], qkv_ref[:, 0:channels], preferred_element_type=F32).astype(BF16)
    for j in range(share):
        span = slice(j * rows, (j + 1) * rows)
        whole = slice(j * 2 * length, (j + 1) * 2 * length)
        context[span, :] = attend_pixel(
            queries[span, :], keyed[whole, 0:channels], keyed[whole, channels : 2 * channels]
        )
    mixed = jnp.dot(context[...], out_weight_ref[...], preferred_element_type=F32)
    for j in range(share):
        for i, k in enumerate(steps):
            for parity in range(2):
                place = 2 * i + parity
                start = pl.multiple_of((me ^ k) * part, part)
                up = up_ref[j, parity, pl.ds(start, part), :].astype(F32)
                first = j * rows + place * part
                out_refs[i][j, parity] = (up + mixed[first : first + part]).astype(BF16)


def attend_first_kernel(
    steps, count, batch, up_ref, stats_ref, gain_ref, block_ref, qkv_ref, out_weight_ref, *refs
):
    *out_refs, normed_ref, keyed, embed, queries, context = refs
    share, _, length, channels = up_ref.shape
    devices = block_ref.shape[0]
    part = length // devices
    frames = 2 * length
    center, scale = moments(stats_ref[...], count, gain_ref[...])
    base = share * part
    for parity in range(2):
        for s in range(devices):
            start = base + parity * part
            embed[parity * length + s * part : parity * length + (s + 1) * part, :] = block_ref[
                s, start : start + part, :
            ].astype(F32)

    def project(first, pixels):
        up = up_ref[pl.ds(first, pixels)].reshape(pixels, frames, channels).astype(F32)
        normed = ((up - center) * scale + embed[...]).astype(BF16).reshape(pixels * frames, channels)
        rows = pl.ds(pl.multiple_of(first * frames, frames), pixels * frames)
        normed_ref[rows, :] = normed
        keyed[rows, :] = jnp.dot(normed, qkv_ref[:, channels:], preferred_element_type=F32).astype(BF16)

    def project_batch(i, carry):
        project(i * batch, batch)
        return carry

    lax.fori_loop(0, share // batch, project_batch, 0)
    if share % batch:
        project(share - share % batch, share % batch)
    attend_targets(steps, up_ref, normed_ref, keyed, qkv_ref, out_weight_ref, out_refs, queries, context)


def attend_rest_kernel(steps, up_ref, normed_ref, keyed, qkv_ref, out_weight_ref, *refs):
    *out_refs, queries, context = refs
    attend_targets(steps, up_ref, normed_ref, keyed, qkv_ref, out_weight_ref, out_refs, queries, context)


def attend_cost(share, length, channels, steps, part):
    rows = share * 2 * part * steps
    flops = 2 * rows * channels * (2 * length * 8 + channels)
    return pl.CostEstimate(flops=flops, bytes_accessed=rows * channels * 4, transcendentals=rows * 8 * length)


def attend_first(steps, up, stats, norm_gain, block, qkv_weight, out_weight):
    share, _, length, channels = up.shape
    devices = block.shape[0]
    part = length // devices
    count = share * 2 * length * (channels // GROUPS)
    rows = share * 2 * length
    piece = jax.ShapeDtypeStruct((share, 2, part, channels), BF16)
    return pl.pallas_call(
        functools.partial(attend_first_kernel, steps, count, 4),
        out_shape=(piece,) * len(steps)
        + (jax.ShapeDtypeStruct((rows, channels), BF16), jax.ShapeDtypeStruct((rows, 2 * channels), BF16)),
        scratch_shapes=[
            pltpu.VMEM((2 * length, channels), F32),
            pltpu.VMEM((share * 2 * part * len(steps), channels), BF16),
            pltpu.VMEM((share * 2 * part * len(steps), channels), BF16),
        ],
        compiler_params=params(40),
        cost_estimate=attend_cost(share, length, channels, len(steps), part),
        name="attend_first",
    )(up, stats, norm_gain.reshape(1, channels), block, qkv_weight, out_weight)


def attend_rest(steps, up, normed, keyed, qkv_weight, out_weight, part):
    share, _, length, channels = up.shape
    piece = jax.ShapeDtypeStruct((share, 2, part, channels), BF16)
    return pl.pallas_call(
        functools.partial(attend_rest_kernel, steps),
        out_shape=(piece,) * len(steps),
        scratch_shapes=[pltpu.VMEM((share * 2 * part * len(steps), channels), BF16)] * 2,
        compiler_params=params(40),
        cost_estimate=attend_cost(share, length, channels, len(steps), part),
        name="attend_rest",
    )(up, normed, keyed, qkv_weight, out_weight)


def unpack_kernel(steps, *refs):
    *block_refs, out_hbm, held, wide, sems = refs
    frames, pixels, _ = held.shape
    pieces = sems.shape[1]
    step = frames // pieces
    copies = []
    share, _, part, _ = block_refs[0].shape
    me = lax.axis_index("frames")
    for half in range(wide.shape[0]):
        lanes = slice(half * LANES, (half + 1) * LANES)
        for k, block_ref in zip(steps, block_refs):
            for j in range(share):
                for parity in range(2):
                    start = parity * pixels + j + (me ^ k) * share
                    rows = block_ref[j, parity, :, lanes].astype(F32)
                    wide[half, pl.ds(start, part, stride=2 * pixels), :] = rows
        for i in range(pieces):
            for f in range(i * step, (i + 1) * step):
                held[f, :, lanes] = wide[half, f * pixels : (f + 1) * pixels, :].astype(BF16)
            span = (pl.ds(i * step, step), slice(None), pl.ds(half * LANES, LANES))
            copies.append(pltpu.make_async_copy(held.at[span], out_hbm.at[span], sems.at[half, i]))
            copies[-1].start()
    for copy in copies:
        copy.wait()


def unpack(steps, blocks):
    share, _, part, channels = blocks[0].shape
    frames, pixels = 2 * part, len(blocks) * share
    return pl.pallas_call(
        functools.partial(unpack_kernel, steps),
        out_shape=jax.ShapeDtypeStruct((frames, pixels, channels), BF16),
        out_specs=pl.BlockSpec(memory_space=pltpu.HBM),
        scratch_shapes=[
            pltpu.VMEM((frames, pixels, channels), BF16),
            pltpu.VMEM((channels // LANES, frames * pixels, LANES), F32),
            pltpu.SemaphoreType.DMA((channels // LANES, 4)),
        ],
        compiler_params=params(24),
        name="unpack_output",
    )(*blocks)


TARGETS = ((4, 2), (6, 7, 5), (1, 3, 0))


def per_device(latent, conv_weight, norm_gain, frame_embed, qkv_weight, out_weight):
    devices = lax.axis_size("frames")
    everyone = devices * lax.axis_size("rows")
    share = latent.shape[1] // devices
    sent = pack(latent, frame_embed, devices)
    block = lax.all_to_all(sent, "frames", 0, 0)
    up, copies = upsample(block, conv_weight, share, everyone)
    stats = lax.all_to_all(copies, ("rows", "frames"), 0, 0)

    def send(piece, k):
        return lax.ppermute(piece, "frames", [(i, i ^ k) for i in range(devices)]) if k else piece

    *pieces, normed, keyed = attend_first(TARGETS[0], up, stats, norm_gain, block, qkv_weight, out_weight)
    got = [send(piece, k) for piece, k in zip(pieces, TARGETS[0])]
    for steps in TARGETS[1:]:
        pieces = attend_rest(steps, up, normed, keyed, qkv_weight, out_weight, pieces[0].shape[2])
        got += [send(piece, k) for piece, k in zip(pieces, steps)]
    return unpack(sum(TARGETS, ()), got)


def solution(mesh):
    return jax.shard_map(
        per_device,
        mesh=mesh,
        in_specs=(P("frames", "rows", None), P(), P(), P("frames", None), P(), P()),
        out_specs=P("frames", "rows", None),
        check_vma=False,
    )
```

```python
import functools

import jax
import jax.numpy as jnp
from jax import lax
from jax.experimental import pallas as pl
from jax.experimental.pallas import tpu as pltpu
from jax.sharding import PartitionSpec as P

HEAD_DIM = 64
GROUPS = 32
EPSILON = 1e-06
LANES = 128
LOG2E = 1.4426950408889634
HIGHEST = lax.Precision.HIGHEST
BF16 = jnp.bfloat16
F32 = jnp.float32
NT = (((1,), (1,)), ((), ()))


def params(mib):
    return pltpu.CompilerParams(vmem_limit_bytes=mib * 1024 * 1024)


def pitch_of(pixels):
    return pixels + 1 - pixels % 2


def pack_kernel(latent_ref, embed_ref, out_ref, wide, embed_wide):
    frames, pixels, _ = latent_ref.shape
    devices = out_ref.shape[0]
    share = pixels // devices
    pitch = pitch_of(pixels)
    for half in range(wide.shape[0]):
        lanes = slice(half * LANES, (half + 1) * LANES)
        for f in range(frames):
            wide[half, f * pitch : f * pitch + pixels, :] = latent_ref[f, :, lanes].astype(F32)
        embed_wide[half, 0 : 2 * frames] = embed_ref[:, lanes].astype(F32)
        for p in range(pixels):
            d, j = divmod(p, share)
            rows = wide[half, pl.ds(p, frames, stride=pitch), :].astype(BF16)
            out_ref[d, j * frames : (j + 1) * frames, lanes] = rows
        for parity in range(2):
            rows = embed_wide[half, pl.ds(parity, frames, stride=2), :].astype(BF16)
            base = share * frames + parity * frames
            for d in range(devices):
                out_ref[d, base : base + frames, lanes] = rows


def pack(latent, frame_embed, devices):
    frames, pixels, channels = latent.shape
    rows = pixels // devices * frames + 2 * frames
    return pl.pallas_call(
        pack_kernel,
        out_shape=jax.ShapeDtypeStruct((devices, rows, channels), BF16),
        scratch_shapes=[
            pltpu.VMEM((channels // LANES, (frames + 1) * pitch_of(pixels), LANES), F32),
            pltpu.VMEM((channels // LANES, 2 * frames + 8, LANES), F32),
        ],
        compiler_params=params(24),
        name="pack_latent",
    )(latent, frame_embed)


def group_matrix(channels, offset):
    size = channels // GROUPS
    channel = lax.broadcasted_iota(jnp.int32, (channels, LANES), 0)
    lane = lax.broadcasted_iota(jnp.int32, (channels, LANES), 1)
    return jnp.where(channel // size + offset == lane, 1.0, 0.0).astype(F32)


def group_spread(channels):
    size = channels // GROUPS
    lane = lax.broadcasted_iota(jnp.int32, (LANES, channels), 0)
    channel = lax.broadcasted_iota(jnp.int32, (LANES, channels), 1)
    return jnp.where(channel // size == lane, 1.0, 0.0).astype(F32)


def exact_dot(a, b):
    return jnp.dot(a, b, precision=HIGHEST, preferred_element_type=F32)


def upsample_kernel(share, block_ref, conv_ref, up_ref, stats_ref, taps):
    devices = block_ref.shape[0]
    channels = block_ref.shape[2]
    part = (block_ref.shape[1]) // (share + 2)
    length = devices * part
    row = lax.broadcasted_iota(jnp.int32, (length, channels), 0)
    for j in range(share):
        here = jnp.concatenate([block_ref[s, j * part : (j + 1) * part, :] for s in range(devices)], axis=0)
        wide = here.astype(F32)
        before = jnp.where(row == 0, 0.0, pltpu.roll(wide, 1, 0))
        after = jnp.where(row == length - 1, 0.0, pltpu.roll(wide, length - 1, 0))
        rows = slice(j * length, (j + 1) * length)
        taps[0, rows, :] = before.astype(BF16)
        taps[1, rows, :] = here
        taps[2, rows, :] = after.astype(BF16)

    count = share * 2 * length * (channels // GROUPS)
    fold = 16

    def column_sums(pieces):
        total = sum(jnp.sum(piece.reshape(-1, fold, channels), axis=0) for piece in pieces)
        return jnp.broadcast_to(jnp.sum(total, axis=0, keepdims=True), (8, channels))

    shifts = jnp.zeros((fold, channels), F32)
    squares = jnp.zeros((fold, channels), F32)
    first = 0
    for pixels in (1, 6, 6):
        rows = slice(first * length, (first + pixels) * length)

        def tap(source, index):
            return jnp.dot(taps[source, rows, :], conv_ref[index], preferred_element_type=F32)

        even = (tap(1, 1) + tap(0, 3)).astype(BF16)
        odd = (tap(2, 0) + tap(1, 2)).astype(BF16)
        if first == 0:
            pivot = column_sums([frames[0:length].astype(F32) for frames in (even, odd)])
            pivot = exact_dot(pivot, group_matrix(channels, 0)) * (share / count)
            center = exact_dot(pivot, group_spread(channels))[0:1]
        for j in range(pixels):
            for parity, frames in enumerate((even, odd)):
                piece = frames[j * length : (j + 1) * length]
                up_ref[first + j, parity] = piece
                away = piece.astype(F32) - center
                shifts += jnp.sum(away.reshape(-1, fold, channels), axis=0)
                squares += jnp.sum((away * away).reshape(-1, fold, channels), axis=0)
        first += pixels
    sums = jnp.concatenate([column_sums([shifts]), column_sums([squares])], axis=0)
    sums = exact_dot(sums, group_matrix(channels, 0))
    shift, square = sums[0:1], sums[8:9]
    own = pivot[0:1] + shift / count + pltpu.roll(square - shift * shift / count, LANES // 2, 1)
    stats_ref[...] = jnp.broadcast_to(own, stats_ref.shape)


def upsample(block, conv_weight, share, copies):
    devices, rows, channels = block.shape
    length = devices * (rows // (share + 2))
    return pl.pallas_call(
        functools.partial(upsample_kernel, share),
        out_shape=(
            jax.ShapeDtypeStruct((share, 2, length, channels), BF16),
            jax.ShapeDtypeStruct((copies, LANES), F32),
        ),
        scratch_shapes=[pltpu.VMEM((3, share * length, channels), BF16)],
        compiler_params=params(48),
        name="upsample",
    )(block, conv_weight)


def moments(stats, count, gain):
    channels = gain.shape[1]
    holders = stats.shape[0]
    center = jnp.sum(stats, axis=0, keepdims=True) / holders
    away = stats - center
    between = jnp.sum(away * away, axis=0, keepdims=True) * count
    within = pltpu.roll(center, LANES // 2, 1) * holders
    lane = lax.broadcasted_iota(jnp.int32, (1, LANES), 1)
    variance = jnp.where(lane < GROUPS, (between + within) / (count * holders), 0.0)
    center = jnp.where(lane < GROUPS, center, 0.0)
    both = jnp.concatenate(
        [jnp.broadcast_to(center, (8, LANES)), jnp.broadcast_to(variance, (8, LANES))], axis=0
    )
    both = exact_dot(both, group_spread(channels))
    return both[0:1], lax.rsqrt(both[8:9] + EPSILON) * gain.astype(F32)


def attend_pixel(queries, keys, values):
    rows, channels = queries.shape
    heads = channels // HEAD_DIM
    head = lax.broadcasted_iota(jnp.int32, (rows, channels), 1) // HEAD_DIM
    first = lax.broadcasted_iota(jnp.int32, (rows, LANES), 1) < HEAD_DIM
    zeros = jnp.zeros_like(queries)
    stacked = jnp.concatenate([jnp.where(head == h, queries, zeros) for h in range(heads)], axis=0)
    scores = lax.dot_general(stacked, keys, NT, preferred_element_type=F32)
    top = jnp.max(scores, axis=1, keepdims=True)
    weights = jnp.exp2((scores - top) * (LOG2E * HEAD_DIM**-0.5))
    scale = 1.0 / jnp.sum(weights, axis=1, keepdims=True)
    mixed = jnp.dot(weights.astype(BF16), values, preferred_element_type=F32)
    context = []
    for pair in range(heads // 2):
        lanes = slice(pair * LANES, (pair + 1) * LANES)
        upper, lower = (slice((2 * pair + i) * rows, (2 * pair + i + 1) * rows) for i in range(2))
        part = jnp.where(first, mixed[upper, lanes], mixed[lower, lanes])
        context.append((part * jnp.where(first, scale[upper], scale[lower])).astype(BF16))
    return jnp.concatenate(context, axis=1)


def attend_targets(steps, up_ref, normed, keyed, qkv_ref, out_weight_ref, out_refs, queries, context):
    share, _, length, channels = up_ref.shape
    part = out_refs[0].shape[2]
    me = lax.axis_index("frames")
    starts = [
        pl.multiple_of(parity * length + (me ^ k) * part, part) for k in steps for parity in range(2)
    ]
    rows = len(starts) * part
    for j in range(share):
        for i, start in enumerate(starts):
            first = j * rows + i * part
            queries[first : first + part, :] = normed[pl.ds(j * 2 * length + start, part), :]
    queries[...] = jnp.dot(queries[...], qkv_ref[:, 0:channels], preferred_element_type=F32).astype(BF16)
    for j in range(share):
        span = slice(j * rows, (j + 1) * rows)
        whole = slice(j * 2 * length, (j + 1) * 2 * length)
        context[span, :] = attend_pixel(
            queries[span, :], keyed[whole, 0:channels], keyed[whole, channels : 2 * channels]
        )
    mixed = jnp.dot(context[...], out_weight_ref[...], preferred_element_type=F32)
    for j in range(share):
        for i, k in enumerate(steps):
            for parity in range(2):
                place = 2 * i + parity
                start = pl.multiple_of((me ^ k) * part, part)
                up = up_ref[j, parity, pl.ds(start, part), :].astype(F32)
                first = j * rows + place * part
                out_refs[i][j, parity] = (up + mixed[first : first + part]).astype(BF16)


def attend_first_kernel(
    steps, count, batch, up_ref, stats_ref, gain_ref, block_ref, qkv_ref, out_weight_ref, *refs
):
    *out_refs, normed_ref, keyed, embed, queries, context = refs
    share, _, length, channels = up_ref.shape
    devices = block_ref.shape[0]
    part = length // devices
    frames = 2 * length
    center, scale = moments(stats_ref[...], count, gain_ref[...])
    base = share * part
    for parity in range(2):
        for s in range(devices):
            start = base + parity * part
            embed[parity * length + s * part : parity * length + (s + 1) * part, :] = block_ref[
                s, start : start + part, :
            ].astype(F32)

    def project(first, pixels):
        up = up_ref[pl.ds(first, pixels)].reshape(pixels, frames, channels).astype(F32)
        normed = ((up - center) * scale + embed[...]).astype(BF16).reshape(pixels * frames, channels)
        rows = pl.ds(pl.multiple_of(first * frames, frames), pixels * frames)
        normed_ref[rows, :] = normed
        keyed[rows, :] = jnp.dot(normed, qkv_ref[:, channels:], preferred_element_type=F32).astype(BF16)

    def project_batch(i, carry):
        project(i * batch, batch)
        return carry

    lax.fori_loop(0, share // batch, project_batch, 0)
    if share % batch:
        project(share - share % batch, share % batch)
    attend_targets(steps, up_ref, normed_ref, keyed, qkv_ref, out_weight_ref, out_refs, queries, context)


def attend_rest_kernel(steps, up_ref, normed_ref, keyed, qkv_ref, out_weight_ref, *refs):
    *out_refs, queries, context = refs
    attend_targets(steps, up_ref, normed_ref, keyed, qkv_ref, out_weight_ref, out_refs, queries, context)


def attend_cost(share, length, channels, steps, part):
    rows = share * 2 * part * steps
    flops = 2 * rows * channels * (2 * length * 8 + channels)
    return pl.CostEstimate(flops=flops, bytes_accessed=rows * channels * 4, transcendentals=rows * 8 * length)


def attend_first(steps, up, stats, norm_gain, block, qkv_weight, out_weight):
    share, _, length, channels = up.shape
    devices = block.shape[0]
    part = length // devices
    count = share * 2 * length * (channels // GROUPS)
    rows = share * 2 * length
    piece = jax.ShapeDtypeStruct((share, 2, part, channels), BF16)
    return pl.pallas_call(
        functools.partial(attend_first_kernel, steps, count, 4),
        out_shape=(piece,) * len(steps)
        + (jax.ShapeDtypeStruct((rows, channels), BF16), jax.ShapeDtypeStruct((rows, 2 * channels), BF16)),
        scratch_shapes=[
            pltpu.VMEM((2 * length, channels), F32),
            pltpu.VMEM((share * 2 * part * len(steps), channels), BF16),
            pltpu.VMEM((share * 2 * part * len(steps), channels), BF16),
        ],
        compiler_params=params(40),
        cost_estimate=attend_cost(share, length, channels, len(steps), part),
        name="attend_first",
    )(up, stats, norm_gain.reshape(1, channels), block, qkv_weight, out_weight)


def attend_rest(steps, up, normed, keyed, qkv_weight, out_weight, part):
    share, _, length, channels = up.shape
    piece = jax.ShapeDtypeStruct((share, 2, part, channels), BF16)
    return pl.pallas_call(
        functools.partial(attend_rest_kernel, steps),
        out_shape=(piece,) * len(steps),
        scratch_shapes=[pltpu.VMEM((share * 2 * part * len(steps), channels), BF16)] * 2,
        compiler_params=params(40),
        cost_estimate=attend_cost(share, length, channels, len(steps), part),
        name="attend_rest",
    )(up, normed, keyed, qkv_weight, out_weight)


def unpack_kernel(steps, *refs):
    *block_refs, out_hbm, held, wide, sems = refs
    frames, pixels, _ = held.shape
    share, _, part, _ = block_refs[0].shape
    pieces = sems.shape[1]
    step = frames // pieces
    pitch = pitch_of(pixels)
    me = lax.axis_index("frames")
    copies = []
    for half in range(wide.shape[0]):
        lanes = slice(half * LANES, (half + 1) * LANES)
        for k, block_ref in zip(steps, block_refs):
            for j in range(share):
                for parity in range(2):
                    start = parity * part * pitch + j + (me ^ k) * share
                    rows = block_ref[j, parity, :, lanes].astype(F32)
                    wide[half, pl.ds(start, part, stride=pitch), :] = rows
        for i in range(pieces):
            for f in range(i * step, (i + 1) * step):
                m, parity = divmod(f, 2)
                first = (parity * part + m) * pitch
                held[f, :, lanes] = wide[half, first : first + pixels, :].astype(BF16)
            span = (pl.ds(i * step, step), slice(None), pl.ds(half * LANES, LANES))
            copies.append(pltpu.make_async_copy(held.at[span], out_hbm.at[span], sems.at[half, i]))
            copies[-1].start()
    for copy in copies:
        copy.wait()


def unpack(steps, blocks):
    share, _, part, channels = blocks[0].shape
    frames, pixels = 2 * part, len(blocks) * share
    return pl.pallas_call(
        functools.partial(unpack_kernel, steps),
        out_shape=jax.ShapeDtypeStruct((frames, pixels, channels), BF16),
        out_specs=pl.BlockSpec(memory_space=pltpu.HBM),
        scratch_shapes=[
            pltpu.VMEM((frames, pixels, channels), BF16),
            pltpu.VMEM((channels // LANES, (frames + 1) * pitch_of(pixels), LANES), F32),
            pltpu.SemaphoreType.DMA((channels // LANES, 4)),
        ],
        compiler_params=params(24),
        name="unpack_output",
    )(*blocks)


TARGETS = ((4, 2), (6, 7, 5), (1, 3, 0))


def per_device(latent, conv_weight, norm_gain, frame_embed, qkv_weight, out_weight):
    devices = lax.axis_size("frames")
    everyone = devices * lax.axis_size("rows")
    share = latent.shape[1] // devices
    sent = pack(latent, frame_embed, devices)
    block = lax.all_to_all(sent, "frames", 0, 0)
    up, copies = upsample(block, conv_weight, share, everyone)
    stats = lax.all_to_all(copies, ("rows", "frames"), 0, 0)

    def send(piece, k):
        return lax.ppermute(piece, "frames", [(i, i ^ k) for i in range(devices)]) if k else piece

    *pieces, normed, keyed = attend_first(TARGETS[0], up, stats, norm_gain, block, qkv_weight, out_weight)
    got = [send(piece, k) for piece, k in zip(pieces, TARGETS[0])]
    for steps in TARGETS[1:]:
        pieces = attend_rest(steps, up, normed, keyed, qkv_weight, out_weight, pieces[0].shape[2])
        got += [send(piece, k) for piece, k in zip(pieces, steps)]
    return unpack(sum(TARGETS, ()), got)


def solution(mesh):
    return jax.shard_map(
        per_device,
        mesh=mesh,
        in_specs=(P("frames", "rows", None), P(), P(), P("frames", None), P(), P()),
        out_specs=P("frames", "rows", None),
        check_vma=False,
    )
```

```python
import functools

import jax
import jax.numpy as jnp
from jax import lax
from jax.experimental import pallas as pl
from jax.experimental.pallas import tpu as pltpu
from jax.sharding import PartitionSpec as P

HEAD_DIM = 64
GROUPS = 32
EPSILON = 1e-06
LANES = 128
LOG2E = 1.4426950408889634
HIGHEST = lax.Precision.HIGHEST
BF16 = jnp.bfloat16
F32 = jnp.float32
NT = (((1,), (1,)), ((), ()))


def params(mib):
    return pltpu.CompilerParams(vmem_limit_bytes=mib * 1024 * 1024)


def pitch_of(pixels):
    return pixels + 1 - pixels % 2


def pack_kernel(latent_ref, embed_ref, out_ref, wide, embed_wide):
    frames, pixels, _ = latent_ref.shape
    devices = out_ref.shape[0]
    share = pixels // devices
    pitch = pitch_of(pixels)
    for half in range(wide.shape[0]):
        lanes = slice(half * LANES, (half + 1) * LANES)
        for f in range(frames):
            wide[half, f * pitch : f * pitch + pixels, :] = latent_ref[f, :, lanes].astype(F32)
        embed_wide[half, 0 : 2 * frames] = embed_ref[:, lanes].astype(F32)
        for p in range(pixels):
            d, j = divmod(p, share)
            rows = wide[half, pl.ds(p, frames, stride=pitch), :].astype(BF16)
            out_ref[d, j * frames : (j + 1) * frames, lanes] = rows
        for parity in range(2):
            rows = embed_wide[half, pl.ds(parity, frames, stride=2), :].astype(BF16)
            base = share * frames + parity * frames
            for d in range(devices):
                out_ref[d, base : base + frames, lanes] = rows


def pack(latent, frame_embed, devices):
    frames, pixels, channels = latent.shape
    rows = pixels // devices * frames + 2 * frames
    return pl.pallas_call(
        pack_kernel,
        out_shape=jax.ShapeDtypeStruct((devices, rows, channels), BF16),
        scratch_shapes=[
            pltpu.VMEM((channels // LANES, (frames + 1) * pitch_of(pixels), LANES), F32),
            pltpu.VMEM((channels // LANES, 2 * frames + 8, LANES), F32),
        ],
        compiler_params=params(24),
        name="pack_latent",
    )(latent, frame_embed)


def group_matrix(channels, offset):
    size = channels // GROUPS
    channel = lax.broadcasted_iota(jnp.int32, (channels, LANES), 0)
    lane = lax.broadcasted_iota(jnp.int32, (channels, LANES), 1)
    return jnp.where(channel // size + offset == lane, 1.0, 0.0).astype(F32)


def group_spread(channels):
    size = channels // GROUPS
    lane = lax.broadcasted_iota(jnp.int32, (LANES, channels), 0)
    channel = lax.broadcasted_iota(jnp.int32, (LANES, channels), 1)
    return jnp.where(channel // size == lane, 1.0, 0.0).astype(F32)


def exact_dot(a, b):
    return jnp.dot(a, b, precision=HIGHEST, preferred_element_type=F32)


def upsample_kernel(share, block_ref, conv_ref, up_ref, stats_ref, taps):
    devices = block_ref.shape[0]
    channels = block_ref.shape[2]
    part = (block_ref.shape[1]) // (share + 2)
    length = devices * part
    row = lax.broadcasted_iota(jnp.int32, (length, channels), 0)
    for j in range(share):
        here = jnp.concatenate([block_ref[s, j * part : (j + 1) * part, :] for s in range(devices)], axis=0)
        wide = here.astype(F32)
        before = jnp.where(row == 0, 0.0, pltpu.roll(wide, 1, 0))
        after = jnp.where(row == length - 1, 0.0, pltpu.roll(wide, length - 1, 0))
        rows = slice(j * length, (j + 1) * length)
        taps[0, rows, :] = before.astype(BF16)
        taps[1, rows, :] = here
        taps[2, rows, :] = after.astype(BF16)

    count = share * 2 * length * (channels // GROUPS)
    fold = 16

    def column_sums(pieces):
        total = sum(jnp.sum(piece.reshape(-1, fold, channels), axis=0) for piece in pieces)
        return jnp.broadcast_to(jnp.sum(total, axis=0, keepdims=True), (8, channels))

    shifts = jnp.zeros((fold, channels), F32)
    squares = jnp.zeros((fold, channels), F32)
    first = 0
    for pixels in (1, 6, 6):
        rows = slice(first * length, (first + pixels) * length)

        def tap(source, index):
            return jnp.dot(taps[source, rows, :], conv_ref[index], preferred_element_type=F32)

        even = (tap(1, 1) + tap(0, 3)).astype(BF16)
        odd = (tap(2, 0) + tap(1, 2)).astype(BF16)
        if first == 0:
            pivot = column_sums([frames[0:length].astype(F32) for frames in (even, odd)])
            pivot = exact_dot(pivot, group_matrix(channels, 0)) * (share / count)
            center = exact_dot(pivot, group_spread(channels))[0:1]
        for j in range(pixels):
            for parity, frames in enumerate((even, odd)):
                piece = frames[j * length : (j + 1) * length]
                up_ref[first + j, parity] = piece
                away = piece.astype(F32) - center
                shifts += jnp.sum(away.reshape(-1, fold, channels), axis=0)
                squares += jnp.sum((away * away).reshape(-1, fold, channels), axis=0)
        first += pixels
    sums = jnp.concatenate([column_sums([shifts]), column_sums([squares])], axis=0)
    sums = exact_dot(sums, group_matrix(channels, 0))
    shift, square = sums[0:1], sums[8:9]
    own = pivot[0:1] + shift / count + pltpu.roll(square - shift * shift / count, LANES // 2, 1)
    stats_ref[...] = jnp.broadcast_to(own, stats_ref.shape)


def upsample(block, conv_weight, share, copies):
    devices, rows, channels = block.shape
    length = devices * (rows // (share + 2))
    return pl.pallas_call(
        functools.partial(upsample_kernel, share),
        out_shape=(
            jax.ShapeDtypeStruct((share, 2, length, channels), BF16),
            jax.ShapeDtypeStruct((copies, LANES), F32),
        ),
        scratch_shapes=[pltpu.VMEM((3, share * length, channels), BF16)],
        compiler_params=params(48),
        name="upsample",
    )(block, conv_weight)


def moments(stats, count, gain):
    channels = gain.shape[1]
    holders = stats.shape[0]
    center = jnp.sum(stats, axis=0, keepdims=True) / holders
    away = stats - center
    between = jnp.sum(away * away, axis=0, keepdims=True) * count
    within = pltpu.roll(center, LANES // 2, 1) * holders
    lane = lax.broadcasted_iota(jnp.int32, (1, LANES), 1)
    variance = jnp.where(lane < GROUPS, (between + within) / (count * holders), 0.0)
    center = jnp.where(lane < GROUPS, center, 0.0)
    both = jnp.concatenate(
        [jnp.broadcast_to(center, (8, LANES)), jnp.broadcast_to(variance, (8, LANES))], axis=0
    )
    both = exact_dot(both, group_spread(channels))
    return both[0:1], lax.rsqrt(both[8:9] + EPSILON) * gain.astype(F32)


def attend_pixel(queries, keys, values):
    rows, channels = queries.shape
    heads = channels // HEAD_DIM
    head = lax.broadcasted_iota(jnp.int32, (rows, channels), 1) // HEAD_DIM
    first = lax.broadcasted_iota(jnp.int32, (rows, LANES), 1) < HEAD_DIM
    zeros = jnp.zeros_like(queries)
    stacked = jnp.concatenate([jnp.where(head == h, queries, zeros) for h in range(heads)], axis=0)
    scores = lax.dot_general(stacked, keys, NT, preferred_element_type=F32)
    top = jnp.max(scores, axis=1, keepdims=True)
    weights = jnp.exp2((scores - top) * (LOG2E * HEAD_DIM**-0.5))
    scale = 1.0 / jnp.sum(weights, axis=1, keepdims=True)
    mixed = jnp.dot(weights.astype(BF16), values, preferred_element_type=F32)
    context = []
    for pair in range(heads // 2):
        lanes = slice(pair * LANES, (pair + 1) * LANES)
        upper, lower = (slice((2 * pair + i) * rows, (2 * pair + i + 1) * rows) for i in range(2))
        part = jnp.where(first, mixed[upper, lanes], mixed[lower, lanes])
        context.append((part * jnp.where(first, scale[upper], scale[lower])).astype(BF16))
    return jnp.concatenate(context, axis=1)


def attend_targets(steps, up_ref, normed, keyed, qkv_ref, out_weight_ref, out_refs, queries, context):
    share, _, length, channels = up_ref.shape
    part = out_refs[0].shape[2]
    me = lax.axis_index("frames")
    starts = [
        pl.multiple_of(parity * length + (me ^ k) * part, part) for k in steps for parity in range(2)
    ]
    rows = len(starts) * part
    for j in range(share):
        for i, start in enumerate(starts):
            first = j * rows + i * part
            queries[first : first + part, :] = normed[pl.ds(j * 2 * length + start, part), :]
    queries[...] = jnp.dot(queries[...], qkv_ref[:, 0:channels], preferred_element_type=F32).astype(BF16)
    for j in range(share):
        span = slice(j * rows, (j + 1) * rows)
        whole = slice(j * 2 * length, (j + 1) * 2 * length)
        context[span, :] = attend_pixel(
            queries[span, :], keyed[whole, 0:channels], keyed[whole, channels : 2 * channels]
        )
    mixed = jnp.dot(context[...], out_weight_ref[...], preferred_element_type=F32)
    for j in range(share):
        for i, k in enumerate(steps):
            for parity in range(2):
                place = 2 * i + parity
                start = pl.multiple_of((me ^ k) * part, part)
                up = up_ref[j, parity, pl.ds(start, part), :].astype(F32)
                first = j * rows + place * part
                out_refs[i][j, parity] = (up + mixed[first : first + part]).astype(BF16)


def attend_first_kernel(
    steps, count, batch, up_ref, stats_ref, gain_ref, block_ref, qkv_ref, out_weight_ref, *refs
):
    *out_refs, normed_ref, keyed, embed, queries, context = refs
    share, _, length, channels = up_ref.shape
    devices = block_ref.shape[0]
    part = length // devices
    frames = 2 * length
    center, scale = moments(stats_ref[...], count, gain_ref[...])
    base = share * part
    for parity in range(2):
        for s in range(devices):
            start = base + parity * part
            embed[parity * length + s * part : parity * length + (s + 1) * part, :] = block_ref[
                s, start : start + part, :
            ].astype(F32)

    def project(first, pixels):
        up = up_ref[pl.ds(first, pixels)].reshape(pixels, frames, channels).astype(F32)
        normed = ((up - center) * scale + embed[...]).astype(BF16).reshape(pixels * frames, channels)
        rows = pl.ds(pl.multiple_of(first * frames, frames), pixels * frames)
        normed_ref[rows, :] = normed
        keyed[rows, :] = jnp.dot(normed, qkv_ref[:, channels:], preferred_element_type=F32).astype(BF16)

    def project_batch(i, carry):
        project(i * batch, batch)
        return carry

    lax.fori_loop(0, share // batch, project_batch, 0)
    if share % batch:
        project(share - share % batch, share % batch)
    attend_targets(steps, up_ref, normed_ref, keyed, qkv_ref, out_weight_ref, out_refs, queries, context)


def attend_rest_kernel(steps, up_ref, normed_ref, keyed, qkv_ref, out_weight_ref, *refs):
    *out_refs, queries, context = refs
    attend_targets(steps, up_ref, normed_ref, keyed, qkv_ref, out_weight_ref, out_refs, queries, context)


def attend_cost(share, length, channels, steps, part):
    rows = share * 2 * part * steps
    flops = 2 * rows * channels * (2 * length * 8 + channels)
    return pl.CostEstimate(flops=flops, bytes_accessed=rows * channels * 4, transcendentals=rows * 8 * length)


def attend_first(steps, up, stats, norm_gain, block, qkv_weight, out_weight):
    share, _, length, channels = up.shape
    devices = block.shape[0]
    part = length // devices
    count = share * 2 * length * (channels // GROUPS)
    rows = share * 2 * length
    piece = jax.ShapeDtypeStruct((share, 2, part, channels), BF16)
    return pl.pallas_call(
        functools.partial(attend_first_kernel, steps, count, 4),
        out_shape=(piece,) * len(steps)
        + (jax.ShapeDtypeStruct((rows, channels), BF16), jax.ShapeDtypeStruct((rows, 2 * channels), BF16)),
        scratch_shapes=[
            pltpu.VMEM((2 * length, channels), F32),
            pltpu.VMEM((share * 2 * part * len(steps), channels), BF16),
            pltpu.VMEM((share * 2 * part * len(steps), channels), BF16),
        ],
        compiler_params=params(40),
        cost_estimate=attend_cost(share, length, channels, len(steps), part),
        name="attend_first",
    )(up, stats, norm_gain.reshape(1, channels), block, qkv_weight, out_weight)


def attend_rest(steps, up, normed, keyed, qkv_weight, out_weight, part):
    share, _, length, channels = up.shape
    piece = jax.ShapeDtypeStruct((share, 2, part, channels), BF16)
    return pl.pallas_call(
        functools.partial(attend_rest_kernel, steps),
        out_shape=(piece,) * len(steps),
        scratch_shapes=[pltpu.VMEM((share * 2 * part * len(steps), channels), BF16)] * 2,
        compiler_params=params(40),
        cost_estimate=attend_cost(share, length, channels, len(steps), part),
        name="attend_rest",
    )(up, normed, keyed, qkv_weight, out_weight)


def unpack_kernel(steps, *refs):
    *block_refs, out_hbm, held, wide, sems = refs
    frames, pixels, _ = held.shape
    share, _, part, _ = block_refs[0].shape
    pieces = sems.shape[1]
    step = frames // pieces
    pitch = pitch_of(pixels)
    me = lax.axis_index("frames")
    copies = []
    for half in range(wide.shape[0]):
        lanes = slice(half * LANES, (half + 1) * LANES)
        for k, block_ref in zip(steps, block_refs):
            for j in range(share):
                for parity in range(2):
                    start = parity * part * pitch + j + (me ^ k) * share
                    rows = block_ref[j, parity, :, lanes].astype(F32)
                    wide[half, pl.ds(start, part, stride=pitch), :] = rows
        for i in range(pieces):
            for f in range(i * step, (i + 1) * step):
                m, parity = divmod(f, 2)
                first = (parity * part + m) * pitch
                held[f, :, lanes] = wide[half, first : first + pixels, :].astype(BF16)
            span = (pl.ds(i * step, step), slice(None), pl.ds(half * LANES, LANES))
            copies.append(pltpu.make_async_copy(held.at[span], out_hbm.at[span], sems.at[half, i]))
            copies[-1].start()
    for copy in copies:
        copy.wait()


def unpack(steps, blocks):
    share, _, part, channels = blocks[0].shape
    frames, pixels = 2 * part, len(blocks) * share
    return pl.pallas_call(
        functools.partial(unpack_kernel, steps),
        out_shape=jax.ShapeDtypeStruct((frames, pixels, channels), BF16),
        out_specs=pl.BlockSpec(memory_space=pltpu.HBM),
        scratch_shapes=[
            pltpu.VMEM((frames, pixels, channels), BF16),
            pltpu.VMEM((channels // LANES, (frames + 1) * pitch_of(pixels), LANES), F32),
            pltpu.SemaphoreType.DMA((channels // LANES, 4)),
        ],
        compiler_params=params(24),
        name="unpack_output",
    )(*blocks)


TARGETS = ((4, 2), (6, 7), (5, 1, 3, 0))


def per_device(latent, conv_weight, norm_gain, frame_embed, qkv_weight, out_weight):
    devices = lax.axis_size("frames")
    everyone = devices * lax.axis_size("rows")
    share = latent.shape[1] // devices
    sent = pack(latent, frame_embed, devices)
    block = lax.all_to_all(sent, "frames", 0, 0)
    up, copies = upsample(block, conv_weight, share, everyone)
    stats = lax.all_to_all(copies, ("rows", "frames"), 0, 0)

    def send(piece, k):
        return lax.ppermute(piece, "frames", [(i, i ^ k) for i in range(devices)]) if k else piece

    *pieces, normed, keyed = attend_first(TARGETS[0], up, stats, norm_gain, block, qkv_weight, out_weight)
    got = [send(piece, k) for piece, k in zip(pieces, TARGETS[0])]
    for steps in TARGETS[1:]:
        pieces = attend_rest(steps, up, normed, keyed, qkv_weight, out_weight, pieces[0].shape[2])
        got += [send(piece, k) for piece, k in zip(pieces, steps)]
    return unpack(sum(TARGETS, ()), got)


def solution(mesh):
    return jax.shard_map(
        per_device,
        mesh=mesh,
        in_specs=(P("frames", "rows", None), P(), P(), P("frames", None), P(), P()),
        out_specs=P("frames", "rows", None),
        check_vma=False,
    )
```

```python
import functools

import jax
import jax.numpy as jnp
from jax import lax
from jax.experimental import pallas as pl
from jax.experimental.pallas import tpu as pltpu
from jax.sharding import PartitionSpec as P

HEAD_DIM = 64
GROUPS = 32
EPSILON = 1e-06
LANES = 128
LOG2E = 1.4426950408889634
HIGHEST = lax.Precision.HIGHEST
BF16 = jnp.bfloat16
F32 = jnp.float32
NT = (((1,), (1,)), ((), ()))


def params(mib):
    return pltpu.CompilerParams(vmem_limit_bytes=mib * 1024 * 1024)


def pitch_of(pixels):
    return pixels + 1 - pixels % 2


def pack_kernel(latent_ref, embed_ref, out_ref, wide, embed_wide):
    frames, pixels, _ = latent_ref.shape
    devices = out_ref.shape[0]
    share = pixels // devices
    pitch = pitch_of(pixels)
    for half in range(wide.shape[0]):
        lanes = slice(half * LANES, (half + 1) * LANES)
        for f in range(frames):
            wide[half, f * pitch : f * pitch + pixels, :] = latent_ref[f, :, lanes].astype(F32)
        embed_wide[half, 0 : 2 * frames] = embed_ref[:, lanes].astype(F32)
        for p in range(pixels):
            d, j = divmod(p, share)
            rows = wide[half, pl.ds(p, frames, stride=pitch), :].astype(BF16)
            out_ref[d, j * frames : (j + 1) * frames, lanes] = rows
        for parity in range(2):
            rows = embed_wide[half, pl.ds(parity, frames, stride=2), :].astype(BF16)
            base = share * frames + parity * frames
            for d in range(devices):
                out_ref[d, base : base + frames, lanes] = rows


def pack(latent, frame_embed, devices):
    frames, pixels, channels = latent.shape
    rows = pixels // devices * frames + 2 * frames
    return pl.pallas_call(
        pack_kernel,
        out_shape=jax.ShapeDtypeStruct((devices, rows, channels), BF16),
        scratch_shapes=[
            pltpu.VMEM((channels // LANES, (frames + 1) * pitch_of(pixels), LANES), F32),
            pltpu.VMEM((channels // LANES, 2 * frames + 8, LANES), F32),
        ],
        compiler_params=params(24),
        name="pack_latent",
    )(latent, frame_embed)


def group_matrix(channels, offset):
    size = channels // GROUPS
    channel = lax.broadcasted_iota(jnp.int32, (channels, LANES), 0)
    lane = lax.broadcasted_iota(jnp.int32, (channels, LANES), 1)
    return jnp.where(channel // size + offset == lane, 1.0, 0.0).astype(F32)


def group_spread(channels):
    size = channels // GROUPS
    lane = lax.broadcasted_iota(jnp.int32, (LANES, channels), 0)
    channel = lax.broadcasted_iota(jnp.int32, (LANES, channels), 1)
    return jnp.where(channel // size == lane, 1.0, 0.0).astype(F32)


def exact_dot(a, b):
    return jnp.dot(a, b, precision=HIGHEST, preferred_element_type=F32)


def upsample_kernel(share, block_ref, conv_ref, up_ref, stats_ref, taps):
    devices = block_ref.shape[0]
    channels = block_ref.shape[2]
    part = (block_ref.shape[1]) // (share + 2)
    length = devices * part
    row = lax.broadcasted_iota(jnp.int32, (length, channels), 0)
    for j in range(share):
        here = jnp.concatenate([block_ref[s, j * part : (j + 1) * part, :] for s in range(devices)], axis=0)
        wide = here.astype(F32)
        before = jnp.where(row == 0, 0.0, pltpu.roll(wide, 1, 0))
        after = jnp.where(row == length - 1, 0.0, pltpu.roll(wide, length - 1, 0))
        rows = slice(j * length, (j + 1) * length)
        taps[0, rows, :] = before.astype(BF16)
        taps[1, rows, :] = here
        taps[2, rows, :] = after.astype(BF16)

    count = share * 2 * length * (channels // GROUPS)
    fold = 16

    def column_sums(pieces):
        total = sum(jnp.sum(piece.reshape(-1, fold, channels), axis=0) for piece in pieces)
        return jnp.broadcast_to(jnp.sum(total, axis=0, keepdims=True), (8, channels))

    shifts = jnp.zeros((fold, channels), F32)
    squares = jnp.zeros((fold, channels), F32)
    first = 0
    for pixels in (1, 6, 6):
        rows = slice(first * length, (first + pixels) * length)

        def tap(source, index):
            return jnp.dot(taps[source, rows, :], conv_ref[index], preferred_element_type=F32)

        even = (tap(1, 1) + tap(0, 3)).astype(BF16)
        odd = (tap(2, 0) + tap(1, 2)).astype(BF16)
        if first == 0:
            pivot = column_sums([frames[0:length].astype(F32) for frames in (even, odd)])
            pivot = exact_dot(pivot, group_matrix(channels, 0)) * (share / count)
            center = exact_dot(pivot, group_spread(channels))[0:1]
        for j in range(pixels):
            for parity, frames in enumerate((even, odd)):
                piece = frames[j * length : (j + 1) * length]
                up_ref[first + j, parity] = piece
                away = piece.astype(F32) - center
                shifts += jnp.sum(away.reshape(-1, fold, channels), axis=0)
                squares += jnp.sum((away * away).reshape(-1, fold, channels), axis=0)
        first += pixels
    sums = jnp.concatenate([column_sums([shifts]), column_sums([squares])], axis=0)
    sums = exact_dot(sums, group_matrix(channels, 0))
    shift, square = sums[0:1], sums[8:9]
    own = pivot[0:1] + shift / count + pltpu.roll(square - shift * shift / count, LANES // 2, 1)
    stats_ref[...] = jnp.broadcast_to(own, stats_ref.shape)


def upsample(block, conv_weight, share, copies):
    devices, rows, channels = block.shape
    length = devices * (rows // (share + 2))
    return pl.pallas_call(
        functools.partial(upsample_kernel, share),
        out_shape=(
            jax.ShapeDtypeStruct((share, 2, length, channels), BF16),
            jax.ShapeDtypeStruct((copies, LANES), F32),
        ),
        scratch_shapes=[pltpu.VMEM((3, share * length, channels), BF16)],
        compiler_params=params(48),
        name="upsample",
    )(block, conv_weight)


def moments(stats, count, gain):
    channels = gain.shape[1]
    holders = stats.shape[0]
    center = jnp.sum(stats, axis=0, keepdims=True) / holders
    away = stats - center
    between = jnp.sum(away * away, axis=0, keepdims=True) * count
    within = pltpu.roll(center, LANES // 2, 1) * holders
    lane = lax.broadcasted_iota(jnp.int32, (1, LANES), 1)
    variance = jnp.where(lane < GROUPS, (between + within) / (count * holders), 0.0)
    center = jnp.where(lane < GROUPS, center, 0.0)
    both = jnp.concatenate(
        [jnp.broadcast_to(center, (8, LANES)), jnp.broadcast_to(variance, (8, LANES))], axis=0
    )
    both = exact_dot(both, group_spread(channels))
    return both[0:1], lax.rsqrt(both[8:9] + EPSILON) * gain.astype(F32)


def attend_pixel(queries, keys, values):
    rows, channels = queries.shape
    heads = channels // HEAD_DIM
    head = lax.broadcasted_iota(jnp.int32, (rows, channels), 1) // HEAD_DIM
    first = lax.broadcasted_iota(jnp.int32, (rows, LANES), 1) < HEAD_DIM
    zeros = jnp.zeros_like(queries)
    stacked = jnp.concatenate([jnp.where(head == h, queries, zeros) for h in range(heads)], axis=0)
    scores = lax.dot_general(stacked, keys, NT, preferred_element_type=F32)
    top = jnp.max(scores, axis=1, keepdims=True)
    weights = jnp.exp2((scores - top) * (LOG2E * HEAD_DIM**-0.5))
    scale = 1.0 / jnp.sum(weights, axis=1, keepdims=True)
    mixed = jnp.dot(weights.astype(BF16), values, preferred_element_type=F32)
    context = []
    for pair in range(heads // 2):
        lanes = slice(pair * LANES, (pair + 1) * LANES)
        upper, lower = (slice((2 * pair + i) * rows, (2 * pair + i + 1) * rows) for i in range(2))
        part = jnp.where(first, mixed[upper, lanes], mixed[lower, lanes])
        context.append((part * jnp.where(first, scale[upper], scale[lower])).astype(BF16))
    return jnp.concatenate(context, axis=1)


def attend_targets(steps, up_ref, normed, keyed, qkv_ref, out_weight_ref, out_refs, queries, context):
    share, _, length, channels = up_ref.shape
    part = out_refs[0].shape[2]
    me = lax.axis_index("frames")
    starts = [
        pl.multiple_of(parity * length + (me ^ k) * part, part) for k in steps for parity in range(2)
    ]
    rows = len(starts) * part
    for j in range(share):
        for i, start in enumerate(starts):
            first = j * rows + i * part
            queries[first : first + part, :] = normed[pl.ds(j * 2 * length + start, part), :]
    queries[...] = jnp.dot(queries[...], qkv_ref[:, 0:channels], preferred_element_type=F32).astype(BF16)
    for j in range(share):
        span = slice(j * rows, (j + 1) * rows)
        whole = slice(j * 2 * length, (j + 1) * 2 * length)
        context[span, :] = attend_pixel(
            queries[span, :], keyed[whole, 0:channels], keyed[whole, channels : 2 * channels]
        )
    mixed = jnp.dot(context[...], out_weight_ref[...], preferred_element_type=F32)
    for j in range(share):
        for i, k in enumerate(steps):
            for parity in range(2):
                place = 2 * i + parity
                start = pl.multiple_of((me ^ k) * part, part)
                up = up_ref[j, parity, pl.ds(start, part), :].astype(F32)
                first = j * rows + place * part
                out_refs[i][j, parity] = (up + mixed[first : first + part]).astype(BF16)


def attend_first_kernel(
    steps, count, batch, up_ref, stats_ref, gain_ref, block_ref, qkv_ref, out_weight_ref, *refs
):
    *out_refs, normed_ref, keyed, embed, queries, context = refs
    share, _, length, channels = up_ref.shape
    devices = block_ref.shape[0]
    part = length // devices
    frames = 2 * length
    center, scale = moments(stats_ref[...], count, gain_ref[...])
    base = share * part
    for parity in range(2):
        for s in range(devices):
            start = base + parity * part
            embed[parity * length + s * part : parity * length + (s + 1) * part, :] = block_ref[
                s, start : start + part, :
            ].astype(F32)

    def project(first, pixels):
        up = up_ref[pl.ds(first, pixels)].reshape(pixels, frames, channels).astype(F32)
        normed = ((up - center) * scale + embed[...]).astype(BF16).reshape(pixels * frames, channels)
        rows = pl.ds(pl.multiple_of(first * frames, frames), pixels * frames)
        normed_ref[rows, :] = normed
        keyed[rows, :] = jnp.dot(normed, qkv_ref[:, channels:], preferred_element_type=F32).astype(BF16)

    def project_batch(i, carry):
        project(i * batch, batch)
        return carry

    lax.fori_loop(0, share // batch, project_batch, 0)
    if share % batch:
        project(share - share % batch, share % batch)
    attend_targets(steps, up_ref, normed_ref, keyed, qkv_ref, out_weight_ref, out_refs, queries, context)


def attend_rest_kernel(steps, up_ref, normed_ref, keyed, qkv_ref, out_weight_ref, *refs):
    *out_refs, queries, context = refs
    attend_targets(steps, up_ref, normed_ref, keyed, qkv_ref, out_weight_ref, out_refs, queries, context)


def attend_cost(share, length, channels, steps, part):
    rows = share * 2 * part * steps
    flops = 2 * rows * channels * (2 * length * 8 + channels)
    return pl.CostEstimate(flops=flops, bytes_accessed=rows * channels * 4, transcendentals=rows * 8 * length)


def attend_first(steps, up, stats, norm_gain, block, qkv_weight, out_weight):
    share, _, length, channels = up.shape
    devices = block.shape[0]
    part = length // devices
    count = share * 2 * length * (channels // GROUPS)
    rows = share * 2 * length
    piece = jax.ShapeDtypeStruct((share, 2, part, channels), BF16)
    return pl.pallas_call(
        functools.partial(attend_first_kernel, steps, count, 4),
        out_shape=(piece,) * len(steps)
        + (jax.ShapeDtypeStruct((rows, channels), BF16), jax.ShapeDtypeStruct((rows, 2 * channels), BF16)),
        scratch_shapes=[
            pltpu.VMEM((2 * length, channels), F32),
            pltpu.VMEM((share * 2 * part * len(steps), channels), BF16),
            pltpu.VMEM((share * 2 * part * len(steps), channels), BF16),
        ],
        compiler_params=params(40),
        cost_estimate=attend_cost(share, length, channels, len(steps), part),
        name="attend_first",
    )(up, stats, norm_gain.reshape(1, channels), block, qkv_weight, out_weight)


def attend_rest(steps, up, normed, keyed, qkv_weight, out_weight, part):
    share, _, length, channels = up.shape
    piece = jax.ShapeDtypeStruct((share, 2, part, channels), BF16)
    return pl.pallas_call(
        functools.partial(attend_rest_kernel, steps),
        out_shape=(piece,) * len(steps),
        scratch_shapes=[pltpu.VMEM((share * 2 * part * len(steps), channels), BF16)] * 2,
        compiler_params=params(40),
        cost_estimate=attend_cost(share, length, channels, len(steps), part),
        name="attend_rest",
    )(up, normed, keyed, qkv_weight, out_weight)


def unpack_kernel(steps, *refs):
    *block_refs, out_hbm, held, wide, sems = refs
    frames, pixels, _ = held.shape
    share, _, part, _ = block_refs[0].shape
    pieces = sems.shape[1]
    step = frames // pieces
    pitch = pitch_of(pixels)
    me = lax.axis_index("frames")
    copies = []
    for half in range(wide.shape[0]):
        lanes = slice(half * LANES, (half + 1) * LANES)
        for k, block_ref in zip(steps, block_refs):
            for j in range(share):
                for parity in range(2):
                    start = parity * part * pitch + j + (me ^ k) * share
                    rows = block_ref[j, parity, :, lanes].astype(F32)
                    wide[half, pl.ds(start, part, stride=pitch), :] = rows
        for i in range(pieces):
            for f in range(i * step, (i + 1) * step):
                m, parity = divmod(f, 2)
                first = (parity * part + m) * pitch
                held[f, :, lanes] = wide[half, first : first + pixels, :].astype(BF16)
            span = (pl.ds(i * step, step), slice(None), pl.ds(half * LANES, LANES))
            copies.append(pltpu.make_async_copy(held.at[span], out_hbm.at[span], sems.at[half, i]))
            copies[-1].start()
    for copy in copies:
        copy.wait()


def unpack(steps, blocks):
    share, _, part, channels = blocks[0].shape
    frames, pixels = 2 * part, len(blocks) * share
    return pl.pallas_call(
        functools.partial(unpack_kernel, steps),
        out_shape=jax.ShapeDtypeStruct((frames, pixels, channels), BF16),
        out_specs=pl.BlockSpec(memory_space=pltpu.HBM),
        scratch_shapes=[
            pltpu.VMEM((frames, pixels, channels), BF16),
            pltpu.VMEM((channels // LANES, (frames + 1) * pitch_of(pixels), LANES), F32),
            pltpu.SemaphoreType.DMA((channels // LANES, 4)),
        ],
        compiler_params=params(24),
        name="unpack_output",
    )(*blocks)


TARGETS = ((4, 2), (6, 7), (5, 1, 3), (0,))


def per_device(latent, conv_weight, norm_gain, frame_embed, qkv_weight, out_weight):
    devices = lax.axis_size("frames")
    everyone = devices * lax.axis_size("rows")
    share = latent.shape[1] // devices
    sent = pack(latent, frame_embed, devices)
    block = lax.all_to_all(sent, "frames", 0, 0)
    up, copies = upsample(block, conv_weight, share, everyone)
    stats = lax.all_to_all(copies, ("rows", "frames"), 0, 0)

    def send(piece, k):
        return lax.ppermute(piece, "frames", [(i, i ^ k) for i in range(devices)]) if k else piece

    *pieces, normed, keyed = attend_first(TARGETS[0], up, stats, norm_gain, block, qkv_weight, out_weight)
    got = [send(piece, k) for piece, k in zip(pieces, TARGETS[0])]
    for steps in TARGETS[1:]:
        pieces = attend_rest(steps, up, normed, keyed, qkv_weight, out_weight, pieces[0].shape[2])
        got += [send(piece, k) for piece, k in zip(pieces, steps)]
    return unpack(sum(TARGETS, ()), got)


def solution(mesh):
    return jax.shard_map(
        per_device,
        mesh=mesh,
        in_specs=(P("frames", "rows", None), P(), P(), P("frames", None), P(), P()),
        out_specs=P("frames", "rows", None),
        check_vma=False,
    )
```
